128 devices in a mesh: shot: 8 (over x, core), rline: 16 (over y, z).
Axes of the slice: x: 4, y: 4, z: 4, core: 2. Of those that a mesh axis runs over, the one named last changes fastest.
Arguments:
- shot_traces: bfloat16 [8, 288, 128, 2048], P('shot', 'rline'), may hold values from -6 to 6
- slot_dest: int32 [8, 288], P('shot', 'rline'), may hold values from 0 to 15, as said below
- slot_offset: int32 [8, 288], P('shot', 'rline'), may hold values from 0 to 8, as said below
- block_count: int32 [8, 16], P('shot', 'rline'), may hold values from 0 to 18, as said below
- amp_index: int32 [8, 288, 128], P('shot', 'rline'), may hold values from 0 to 1023
- amp_table: float32 [1024], P('shot'), may hold values from 0.1 to 0.6
- dip_trace: bfloat16 [8, 32], replicated, may hold values from -1 to 1
- dip_time: bfloat16 [8, 64], replicated, may hold values from -0.25 to 0.25
Outputs:
- filtered: bfloat16 [8, 288, 128, 2048], P('shot', 'rline')
The draws below stay inside these ranges and needn't reach their ends.
Inputs may be any that keep to these rules, and one draw needn't show every extreme that they name: Within each shot row, every pair (slot_dest, slot_offset) is named by exactly one live slot; a device's live slots name one destination at most 2 times, and some device names one destination exactly 2 times. The devices at rline indices 2m and 2m + 1 together hold 18 live slots; of the one holding more (either when equal), the first 9 slots name one destination at most 1 times, and so do its live slots from 9 on together with the other device's live slots; some such set names one destination exactly 1 times. Dead slots hold 0. `slot_offset`: dead slots hold 0. `block_count`: each shot row's counts sum to 144, and those of rline indices 2m and 2m + 1 to 18; in every row some device holds exactly 18 live slots and some holds none.
All inputs are finite; a program needn't handle non-finite values.
Results may differ from the reference program's by a relative error of at most 0.0034.
Values may be sent and summed in bfloat16 or wider, within the bound.
No kernel may reach another device: no remote copies, remote signals or barrier semaphores. Data moves between devices by JAX's collectives and lax.ppermute only.
A program may use at most 128 MiB of HBM per device.

```python
import math
import jax
import jax.numpy as jnp
from jax import lax

NT = 2048
BLOCK = 128
TAPS_T = 64
TAPS_X = 32
DIPS = 8
RB = 9
SLOTS = 18
TABLE = 1024
N_SHOT = 8
N_RLINE = 16


def survey_layout(key):
    slot_total = 2 * RB

    def one_row(row_key):
        row_keys = jax.random.split(row_key, 6)
        pair_order = jax.random.permutation(row_keys[0], N_RLINE // 2).astype(jnp.int32)
        flip = jax.random.randint(row_keys[5], (N_RLINE // 2,), 0, 2).astype(jnp.int32)
        member = jnp.arange(N_RLINE, dtype=jnp.int32) % 2
        pair_of = jnp.arange(N_RLINE, dtype=jnp.int32) // 2
        source_order = 2 * pair_order[pair_of] + (member ^ flip[pair_of])
        spread = jax.random.randint(row_keys[1], (N_RLINE // 2,), 0, RB + 1)
        chosen = jax.random.randint(row_keys[2], (), 0, N_RLINE // 2)
        spread = jnp.where(jnp.arange(N_RLINE // 2) == chosen, RB, spread)
        in_order = jnp.stack([RB + spread, RB - spread], axis=1).reshape(-1).astype(jnp.int32)
        starts = jnp.cumsum(in_order) - in_order
        slot_ids = jnp.arange(slot_total, dtype=jnp.int32)
        global_pos = starts[:, None] + slot_ids[None, :]
        live_slot = slot_ids[None, :] < in_order[:, None]
        relabel = jax.random.permutation(row_keys[3], N_RLINE).astype(jnp.int32)
        shuffles = jax.vmap(lambda sub_key: jax.random.permutation(sub_key, RB))(jax.random.split(row_keys[4], N_RLINE)).astype(jnp.int32)
        raw_dest = global_pos % N_RLINE
        raw_pos = jnp.minimum(global_pos // N_RLINE, RB - 1)
        destination = jnp.where(live_slot, relabel[raw_dest], 0)
        position = jnp.where(live_slot, shuffles[raw_dest, raw_pos], 0)
        dest_source = jnp.zeros_like(destination).at[source_order].set(destination)
        pos_source = jnp.zeros_like(position).at[source_order].set(position)
        count_source = jnp.zeros_like(in_order).at[source_order].set(in_order)
        return (dest_source.reshape(-1), pos_source.reshape(-1), count_source)
    return jax.vmap(one_row)(jax.random.split(key, N_SHOT))


def draw_slot_dest(key, part):
    return survey_layout(key)[0].astype(jnp.int32)


def draw_slot_offset(key, part):
    return survey_layout(key)[1].astype(jnp.int32)


def draw_block_count(key, part):
    return survey_layout(key)[2].astype(jnp.int32)


def place_ends(entries, rng, low, top_value):
    spot = [jax.random.randint(jax.random.fold_in(rng, axis), (), 0, length) for axis, length in enumerate(entries.shape)]
    longest = entries.shape.index(max(entries.shape))
    neighbour = spot[:longest] + [(spot[longest] + 1) % entries.shape[longest]] + spot[longest + 1:]
    return entries.at[tuple(spot)].set(low).at[tuple(neighbour)].set(top_value)


def block_scale(rng, dims, pieces, smallest, high):
    factor_of = 1.0
    for dim, shards_of in pieces:
        steps = jax.random.uniform(jax.random.fold_in(jax.random.fold_in(rng, 6), dim), (shards_of,), jnp.float32, smallest / len(pieces), high / len(pieces))
        factor_of = factor_of * jnp.repeat(jnp.exp(steps), dims[dim] // shards_of).reshape((-1,) + (1,) * (len(dims) - 1 - dim))
    return factor_of


def noise(stream_key, extent, width, most, cuts=(), kind=jnp.bfloat16):
    entries = jax.random.normal(stream_key, extent, jnp.float32) * width
    if len(cuts) > 0:
        entries = block_scale(stream_key, extent, cuts, -0.22, 0.18) * entries
    return jnp.clip(entries, min=-most, max=most).astype(kind)


def setup_inputs(seed: int = 0) -> dict:
    key_list = jax.random.split(jax.random.key(seed), 9)
    return {
        "shot_traces": noise(key_list[0], (N_SHOT, N_RLINE * SLOTS, BLOCK, NT), 1.0, 6.0, ((0, 8), (1, 16))),
        "slot_dest": draw_slot_dest(jax.random.fold_in(key_list[8], 71), 0),
        "slot_offset": draw_slot_offset(jax.random.fold_in(key_list[8], 71), 0),
        "block_count": draw_block_count(jax.random.fold_in(key_list[8], 71), 0),
        "amp_index": place_ends(jax.random.randint(key_list[4], (N_SHOT, N_RLINE * SLOTS, BLOCK), 0, TABLE), jax.random.fold_in(key_list[4], 1), 0, TABLE - 1).astype(jnp.int32),
        "amp_table": jnp.clip(jnp.exp(math.log(0.6) - 1.7917595 * jax.random.uniform(key_list[5], (TABLE,), jnp.float32) ** block_scale(key_list[5], (TABLE,), ((0, 8),), -0.2, 0.2)), 0.1, 0.6),
        "dip_trace": noise(key_list[6], (DIPS, TAPS_X), TAPS_X ** -0.5, 1.0),
        "dip_time": noise(key_list[7], (DIPS, TAPS_T), (TAPS_T * DIPS) ** -0.5, 0.25),
    }


tile_len = 128


def band_matrix(tap_values, out_len, in_len, shift):
    tap_total = tap_values.shape[1]
    row_grid = lax.broadcasted_iota(jnp.int32, (out_len, in_len), 0)
    col_grid = lax.broadcasted_iota(jnp.int32, (out_len, in_len), 1)
    tap_index = col_grid + shift - row_grid
    onehot = (tap_index[None, :, :] == jnp.arange(tap_total, dtype=jnp.int32)[:, None, None]).astype(jnp.float32)
    return jnp.einsum("ck,kiu->ciu", tap_values.astype(jnp.float32), onehot, precision=lax.Precision.HIGHEST).astype(jnp.bfloat16)


def filter_block(padded, weights, block_idx, matrices):
    trace_main, trace_tail, time_main, time_tail = matrices
    dip_total = trace_main.shape[0]
    block_len = trace_main.shape[1]
    taps_x = trace_tail.shape[2]
    taps_t = time_tail.shape[2]
    sample_total = padded.shape[1]
    window = lax.dynamic_slice_in_dim(padded, block_idx * block_len, block_len + taps_x, 0).astype(jnp.float32)
    trace_pass = jnp.einsum("ciu,ut->cit", trace_main.astype(jnp.float32), window[:block_len], precision=lax.Precision.HIGHEST)
    trace_pass = trace_pass + jnp.einsum("ciu,ut->cit", trace_tail.astype(jnp.float32), window[block_len:], precision=lax.Precision.HIGHEST)
    trace_pass = trace_pass.astype(jnp.bfloat16)
    time_padded = jnp.pad(trace_pass, ((0, 0), (0, 0), (taps_t // 2, tile_len - taps_t // 2)))
    time_padded = time_padded.reshape(dip_total, block_len, sample_total // tile_len + 1, tile_len).astype(jnp.float32)
    time_pass = jnp.einsum("crbu,ciu->rbi", time_padded[:, :, :-1], time_main.astype(jnp.float32), precision=lax.Precision.HIGHEST)
    time_pass = time_pass + jnp.einsum("crbu,ciu->rbi", time_padded[:, :, 1:, :taps_t], time_tail.astype(jnp.float32), precision=lax.Precision.HIGHEST)
    weight = lax.dynamic_slice_in_dim(weights, block_idx * block_len, block_len, 0)
    center = window[taps_x // 2:taps_x // 2 + block_len]
    return (center - weight[:, None] * time_pass.reshape(block_len, sample_total)).astype(jnp.bfloat16)


def reference(shot_traces, slot_dest, slot_offset, block_count, amp_index, amp_table, dip_trace, dip_time):
    slot_total = 2 * RB
    matrices = (band_matrix(dip_trace, BLOCK, BLOCK, 0), band_matrix(dip_trace, BLOCK, TAPS_X, BLOCK),
                band_matrix(dip_time, tile_len, tile_len, 0), band_matrix(dip_time, tile_len, TAPS_T, tile_len))
    trace_weight = amp_table[amp_index]
    slot_ids = jnp.arange(N_RLINE * slot_total, dtype=jnp.int32)
    owner = slot_ids // slot_total
    live_mask = (slot_ids % slot_total)[None, :] < block_count[:, owner]
    target = jnp.where(live_mask, slot_dest * RB + slot_offset, N_RLINE * RB).astype(jnp.int32)
    half_x = TAPS_X // 2
    row_outputs = []
    for shot_row in range(N_SHOT):
        blocks = jnp.zeros((N_RLINE * RB, BLOCK, NT), jnp.bfloat16).at[target[shot_row]].set(shot_traces[shot_row], mode="drop")
        recv_weights = jnp.zeros((N_RLINE * RB, BLOCK), jnp.float32).at[target[shot_row]].set(trace_weight[shot_row], mode="drop")
        line_rows = blocks.reshape(N_RLINE * RB * BLOCK, NT)
        padded = jnp.pad(line_rows, ((half_x, BLOCK - half_x), (0, 0)))
        weights = recv_weights.reshape(-1)
        cleaned = lax.map(lambda block_idx: filter_block(padded, weights, block_idx, matrices),
                          jnp.arange(N_RLINE * RB, dtype=jnp.int32))
        returned = jnp.take(cleaned, jnp.minimum(target[shot_row], N_RLINE * RB - 1), axis=0)
        returned = jnp.where(live_mask[shot_row][:, None, None], returned, jnp.zeros_like(returned))
        row_outputs.append(returned)
    return jnp.stack(row_outputs)
```

```python
import functools

import jax
import jax.numpy as jnp
from jax import lax
from jax.experimental import pallas as pl
from jax.experimental.pallas import tpu as pltpu
from jax.sharding import PartitionSpec as P

BF16 = jnp.bfloat16
F32 = jnp.float32
EDGE = 16
TILE = 256
VMEM_LIMIT = 56 * 2**20


def time_matrix(dip_time):
    dips, taps = dip_time.shape
    row = lax.broadcasted_iota(jnp.int32, (256, 128), 0)
    col = lax.broadcasted_iota(jnp.int32, (256, 128), 1)
    hit = (row - col)[None] == jnp.arange(taps, dtype=jnp.int32)[:, None, None]
    values = dip_time.astype(F32)[:, :, None, None]
    band = jnp.sum(jnp.where(hit[None], values, F32(0.0)), axis=1).astype(BF16)
    zero = jnp.zeros((dips, 128, 128), BF16)
    main = jnp.concatenate([band, jnp.concatenate([zero, band[:, :128]], axis=1)], axis=2)
    tail = jnp.concatenate([zero, band[:, 128:]], axis=2)
    return jnp.concatenate([main.reshape(dips * 256, 256), tail.reshape(dips * 128, 256)], axis=0)


def trace_matrix(dip_trace, starts, width):
    dips, taps = dip_trace.shape
    rows = starts.shape[0]
    col = lax.broadcasted_iota(jnp.int32, (rows, width), 1)
    hit = (col - starts[:, None])[None] == jnp.arange(taps, dtype=jnp.int32)[:, None, None]
    values = dip_trace.astype(F32)[:, :, None, None]
    band = jnp.sum(jnp.where(hit[None], values, F32(0.0)), axis=1).astype(BF16)
    return band.reshape(dips * rows, width)


def time_lhs(tp, dips, rows, tile):
    base = tile * TILE
    parts = [tp[c * rows : (c + 1) * rows, base : base + 256] for c in range(dips)]
    parts += [tp[c * rows : (c + 1) * rows, base + 256 : base + 384] for c in range(dips)]
    return jnp.concatenate(parts, axis=1)


def interior_kernel(dips, half_t, count, x, w, xi, m, *refs):
    o, shifted, tp = refs[-3:]
    rows = x.shape[1] - 2 * EDGE
    samples = x.shape[2]
    slot = pl.program_id(0) + count[1]

    @pl.when(pl.program_id(0) == 0)
    def _():
        shifted[...] = jnp.zeros_like(shifted)

    @pl.when(slot < count[0])
    def _():
        shifted[:, half_t : half_t + samples] = x[0]
        for lo in range(0, samples + 128, TILE):
            hi = min(lo + TILE, samples + 128)
            tp[:, lo:hi] = jnp.dot(
                xi[...], shifted[:, lo:hi], preferred_element_type=F32
            ).astype(BF16)
        for tile in range(samples // TILE):
            cols = slice(tile * TILE, (tile + 1) * TILE)
            noise = jnp.dot(
                time_lhs(tp, dips, rows, tile), m[...], preferred_element_type=F32
            )
            weight = jnp.concatenate([w[0, EDGE : EDGE + rows]] * 2, axis=1)
            center = x[0, EDGE : EDGE + rows, cols].astype(F32)
            o[0, EDGE : EDGE + rows, cols] = (center - weight * noise).astype(BF16)

    @pl.when(slot >= count[0])
    def _():
        o[...] = jnp.zeros_like(o)


def interior(count, x, w, xi, m, start, steps, out=None):
    slots, block, samples = x.shape
    dips = m.shape[0] // 384
    fetch = lambda i, n: (jnp.minimum(i + n[1], jnp.maximum(n[0] - 1, 0)), 0, 0)
    in_specs = [
        pl.BlockSpec((1, block, samples), fetch),
        pl.BlockSpec((1, block, 128), fetch),
        pl.BlockSpec(xi.shape, lambda i, n: (0, 0)),
        pl.BlockSpec(m.shape, lambda i, n: (0, 0)),
    ]
    args = [jnp.stack([count, jnp.int32(start)]), x, w, xi, m]
    aliases = {}
    if out is not None:
        in_specs.append(pl.BlockSpec(memory_space=pl.ANY))
        args.append(out)
        aliases = {5: 0}
    return pl.pallas_call(
        functools.partial(interior_kernel, dips, 32),
        out_shape=jax.ShapeDtypeStruct(x.shape, BF16),
        grid_spec=pltpu.PrefetchScalarGridSpec(
            num_scalar_prefetch=1,
            grid=(steps,),
            in_specs=in_specs,
            out_specs=pl.BlockSpec((1, block, samples), lambda i, n: (i + n[1], 0, 0)),
            scratch_shapes=[
                pltpu.VMEM((block, samples + 128), BF16),
                pltpu.VMEM((xi.shape[0], samples + 128), BF16),
            ],
        ),
        input_output_aliases=aliases,
        compiler_params=pltpu.CompilerParams(
            dimension_semantics=("arbitrary",), vmem_limit_bytes=VMEM_LIMIT
        ),
        cost_estimate=pl.CostEstimate(
            flops=steps * 8_000_000_000, bytes_accessed=steps * 2**20, transcendentals=0
        ),
        name="interior",
    )(*args)


def edge_kernel(dips, half_t, groups, count, xt, xb, halo, w, xe, m, _, o, shifted, tp, res, sems):
    g = pl.program_id(0)
    per = xt.shape[0]
    samples = xt.shape[2]
    rows = per * 2 * EDGE
    n_slices = halo.shape[0]
    live = g * per < count[0]

    def copies(group):
        slots = pl.ds(group * per, per)
        return (
            pltpu.make_async_copy(
                res.at[group, :, pl.ds(0, EDGE)], o.at[slots, pl.ds(0, EDGE)], sems.at[group, 0]
            ),
            pltpu.make_async_copy(
                res.at[group, :, pl.ds(EDGE, EDGE)],
                o.at[slots, pl.ds(128 - EDGE, EDGE)],
                sems.at[group, 1],
            ),
        )

    @pl.when(g == 0)
    def _():
        shifted[...] = jnp.zeros_like(shifted)

    @pl.when(live)
    def _():
        for i in range(per):
            above = jnp.concatenate([halo[s, i, :EDGE] for s in range(n_slices)], axis=1)
            below = jnp.concatenate([halo[s, i, EDGE:] for s in range(n_slices)], axis=1)
            here = slice(half_t, half_t + samples)
            shifted[i, 0:16, here] = above
            shifted[i, 16:48, here] = xt[i]
            shifted[i, 48:80, here] = xb[i]
            shifted[i, 80:96, here] = below
            for lo in range(0, samples + 128, TILE):
                hi = min(lo + TILE, samples + 128)
                part = jnp.dot(xe[...], shifted[i, :, lo:hi], preferred_element_type=F32)
                part = part.astype(BF16)
                for c in range(dips):
                    tp[c * rows + i * 32 : c * rows + i * 32 + 32, lo:hi] = part[c * 32 : c * 32 + 32]
        for tile in range(samples // TILE):
            cols = slice(tile * TILE, (tile + 1) * TILE)
            noise = jnp.dot(
                time_lhs(tp, dips, rows, tile), m[...], preferred_element_type=F32
            )
            for i in range(per):
                keep = g * per + i < count[0]
                top = noise[i * 32 : i * 32 + 16]
                bottom = noise[i * 32 + 16 : i * 32 + 32]
                wt = jnp.concatenate([w[i, :EDGE]] * 2, axis=1)
                wb = jnp.concatenate([w[i, 128 - EDGE :]] * 2, axis=1)
                top = xt[i, :EDGE, cols].astype(F32) - wt * top
                bottom = xb[i, EDGE:, cols].astype(F32) - wb * bottom
                res[g, i, :EDGE, cols] = jnp.where(keep, top, 0.0).astype(BF16)
                res[g, i, EDGE:, cols] = jnp.where(keep, bottom, 0.0).astype(BF16)
        for copy in copies(g):
            copy.start()

    @pl.when(g == groups - 1)
    def _():
        for group in range(groups):

            @pl.when(group * per < count[0])
            def _():
                for copy in copies(group):
                    copy.wait()


def edges(count, x, halo, w, xe, m, out, per=6):
    slots, block, samples = x.shape
    dips = m.shape[0] // 384
    groups = slots // per
    last = lambda g, n: jnp.minimum(g, jnp.maximum(n[0] - 1, 0) // per)
    return pl.pallas_call(
        functools.partial(edge_kernel, dips, 32, groups),
        out_shape=jax.ShapeDtypeStruct(x.shape, BF16),
        grid_spec=pltpu.PrefetchScalarGridSpec(
            num_scalar_prefetch=1,
            grid=(groups,),
            in_specs=[
                pl.BlockSpec((per, 32, samples), lambda g, n: (last(g, n), 0, 0)),
                pl.BlockSpec((per, 32, samples), lambda g, n: (last(g, n), 3, 0)),
                pl.BlockSpec((halo.shape[0], per, 32, 128), lambda g, n: (0, last(g, n), 0, 0)),
                pl.BlockSpec((per, block, 128), lambda g, n: (last(g, n), 0, 0)),
                pl.BlockSpec(xe.shape, lambda g, n: (0, 0)),
                pl.BlockSpec(m.shape, lambda g, n: (0, 0)),
                pl.BlockSpec(memory_space=pl.ANY),
            ],
            out_specs=pl.BlockSpec(memory_space=pl.ANY),
            scratch_shapes=[
                pltpu.VMEM((per, 96, samples + 128), BF16),
                pltpu.VMEM((dips * per * 32, samples + 128), BF16),
                pltpu.VMEM((groups, per, 32, samples), BF16),
                pltpu.SemaphoreType.DMA((groups, 2)),
            ],
        ),
        input_output_aliases={7: 0},
        compiler_params=pltpu.CompilerParams(
            dimension_semantics=("arbitrary",), vmem_limit_bytes=VMEM_LIMIT
        ),
        cost_estimate=pl.CostEstimate(
            flops=8_000_000_000, bytes_accessed=2**23, transcendentals=0
        ),
        name="edges",
    )(count.reshape(1), x, x, halo, w, xe, m, out)


def permute_kernel(before, after, x, o):
    total = x.shape[0]

    def step(q, _):
        a = before[q]
        b = after[q]
        above = x[jnp.maximum(a, 0), EDGE:]
        below = x[jnp.maximum(b, 0), :EDGE]
        o[q, :EDGE] = jnp.where(a >= 0, above, jnp.zeros_like(above))
        o[q, EDGE:] = jnp.where(b >= 0, below, jnp.zeros_like(below))
        return 0

    lax.fori_loop(0, total, step, 0, unroll=8)


def permute(before, after, x):
    return pl.pallas_call(
        permute_kernel,
        out_shape=jax.ShapeDtypeStruct(x.shape, BF16),
        grid_spec=pltpu.PrefetchScalarGridSpec(
            num_scalar_prefetch=2,
            grid=(1,),
            in_specs=[pl.BlockSpec(x.shape, lambda i, a, b: (0, 0, 0))],
            out_specs=pl.BlockSpec(x.shape, lambda i, a, b: (0, 0, 0)),
        ),
        compiler_params=pltpu.CompilerParams(vmem_limit_bytes=VMEM_LIMIT),
        cost_estimate=pl.CostEstimate(flops=0, bytes_accessed=2**23, transcendentals=0),
        name="permute",
    )(before, after, x)


def shards(
    shot_traces, slot_dest, slot_offset, block_count, amp_index, amp_table, dip_trace, dip_time
):
    x = shot_traces[0]
    slots, block, samples = x.shape
    lines = lax.axis_size("rline")
    per_line = slots // 2
    width = samples // lines
    count = block_count[0, 0]
    slot_ids = jnp.arange(slots, dtype=jnp.int32)
    place = jnp.where(slot_ids < count, slot_dest[0] * per_line + slot_offset[0], -2)

    ends = jnp.concatenate([x[:, :EDGE], x[:, block - EDGE :]], axis=1)
    ends = ends.reshape(slots, 2 * EDGE, lines, width).transpose(2, 0, 1, 3)
    slice_ends = lax.all_to_all(ends, "rline", split_axis=0, concat_axis=0, tiled=True)

    places = lax.all_gather(place, "rline", axis=0, tiled=True)
    amps = lax.all_gather(amp_table, "shot", axis=0, tiled=True)
    ids = jnp.arange(places.shape[0], dtype=jnp.int32)[None, :]
    difference = places[None, :] - places[:, None]
    known = (places >= 0)[:, None] & (places >= 0)[None, :]
    before = jnp.max(jnp.where(known & (difference == -1), ids, -1), axis=1)
    after = jnp.max(jnp.where(known & (difference == 1), ids, -1), axis=1)

    table_hit = amp_index[0][:, :, None] == jnp.arange(amps.shape[0], dtype=jnp.int32)
    weight = jnp.sum(jnp.where(table_hit, amps, F32(0.0)), axis=2)
    weight = jnp.broadcast_to(weight[:, :, None], (slots, block, 128))

    m = time_matrix(dip_time)
    rows = jnp.arange(block - 2 * EDGE, dtype=jnp.int32)
    xi = trace_matrix(dip_trace, rows, block)
    edge_rows = jnp.arange(2 * EDGE, dtype=jnp.int32)
    xe = trace_matrix(dip_trace, jnp.where(edge_rows < EDGE, edge_rows, edge_rows + 32), 96)

    half = slots // 2
    out = interior(count, x, weight, xi, m, 0, half)
    flat = slice_ends.reshape(lines * slots, 2 * EDGE, width)
    moved = permute(before, after, flat).reshape(lines, slots, 2 * EDGE, width)
    halo = lax.all_to_all(moved, "rline", split_axis=0, concat_axis=0, tiled=True)
    out = interior(count, x, weight, xi, m, half, half, out)
    out = edges(count, x, halo, weight, xe, m, out)
    return out[None]


def solution(mesh):
    in_specs = (
        P("shot", "rline", None, None),
        P("shot", "rline"),
        P("shot", "rline"),
        P("shot", "rline"),
        P("shot", "rline", None),
        P("shot"),
        P(),
        P(),
    )
    out_specs = P("shot", "rline", None, None)
    return jax.shard_map(shards, mesh=mesh, in_specs=in_specs, out_specs=out_specs, check_vma=False)
```

```python
import functools

import jax
import jax.numpy as jnp
from jax import lax
from jax.experimental import pallas as pl
from jax.experimental.pallas import tpu as pltpu
from jax.sharding import PartitionSpec as P

BF16 = jnp.bfloat16
F32 = jnp.float32
EDGE = 16
TILE = 256
HALF_T = 32
PAIR_K = 640
VMEM_LIMIT = 56 * 2**20
FIRST = 7


def params(limit=VMEM_LIMIT):
    return pltpu.CompilerParams(dimension_semantics=("arbitrary",), vmem_limit_bytes=limit)


def cost(flops, bytes_accessed):
    return pl.CostEstimate(flops=flops, bytes_accessed=bytes_accessed, transcendentals=0)


def dip_order(dips):
    return list(range(0, dips, 2)) + list(range(1, dips, 2))


def matrices_kernel(taps_x, taps_t, m, xi, xe):
    dips = taps_x.shape[0]
    row = lax.broadcasted_iota(jnp.int32, (TILE, TILE), 0)
    col = lax.broadcasted_iota(jnp.int32, (TILE, TILE), 1)
    for c in range(dips):
        base = jnp.broadcast_to(taps_t[c : c + 1], (TILE, TILE))
        band = pltpu.roll(base, 0, 1, stride=1, stride_axis=0)
        at = c * (PAIR_K // 2)
        m[at : at + TILE] = jnp.where(col <= row, band, 0.0).astype(BF16)
        m[at + TILE : at + PAIR_K // 2] = jnp.where(col > row, band, 0.0)[:64].astype(BF16)
    rows = xi.shape[0] // dips
    for i, c in enumerate(dip_order(dips)):
        base = jnp.broadcast_to(taps_x[c : c + 1], (rows, 128))
        band = pltpu.roll(base, 0, 1, stride=1, stride_axis=0)
        xi[i * rows : (i + 1) * rows] = band.astype(BF16)
        xe[i * 32 : i * 32 + 16] = band[:16, :96].astype(BF16)
        xe[i * 32 + 16 : i * 32 + 32] = band[48:64, :96].astype(BF16)


def matrices(dip_trace, dip_time, rows):
    dips, taps = dip_time.shape
    taps_x = jnp.pad(dip_trace.astype(F32), ((0, 0), (0, 128 - dip_trace.shape[1])))
    taps_t = dip_time.astype(F32)
    gap = jnp.zeros((dips, TILE - taps), F32)
    taps_t = jnp.concatenate([taps_t[:, :1], gap, taps_t[:, :0:-1]], axis=1)
    return pl.pallas_call(
        matrices_kernel,
        out_shape=(
            jax.ShapeDtypeStruct((dips * PAIR_K // 2, TILE), BF16),
            jax.ShapeDtypeStruct((dips * rows, 128), BF16),
            jax.ShapeDtypeStruct((dips * 32, 96), BF16),
        ),
        compiler_params=pltpu.CompilerParams(vmem_limit_bytes=16 * 2**20),
        cost_estimate=cost(0, 2**21),
        name="matrices",
    )(taps_x, taps_t)


def time_lhs(tp, dips, rows, tile):
    base = tile * TILE
    low = lax.broadcasted_iota(jnp.int32, (rows, 128), 1) < 64
    parts = []
    for pair in range(dips // 2):
        even = pl.ds(pair * rows, rows)
        odd = pl.ds((dips // 2 + pair) * rows, rows)
        parts.append(tp[even, base : base + 256])
        parts.append(jnp.where(low, tp[even, base + 256 : base + 384], tp[odd, base : base + 128]))
        parts.append(tp[odd, base + 128 : base + 384])
    return jnp.concatenate(parts, axis=1)


def noise_tiles(tp, m, dips, rows, tiles):
    lhs = jnp.concatenate([time_lhs(tp, dips, rows, tile) for tile in tiles], axis=0)
    noise = jnp.dot(lhs, m[...], preferred_element_type=F32)
    return [noise[k * rows : (k + 1) * rows] for k in range(len(tiles))]


def column_tiles(samples):
    return [(lo, min(lo + TILE, samples + 128)) for lo in range(0, samples + 128, TILE)]


def interior_kernel(dips, count, x, w, xi, m, *refs):
    o, shifted, tp = refs[-3:]
    rows = x.shape[1] - 2 * EDGE
    samples = x.shape[2]
    half = dips // 2 * rows
    slot = pl.program_id(0) + count[1]

    @pl.when(pl.program_id(0) == 0)
    def _():
        shifted[...] = jnp.zeros_like(shifted)

    @pl.when(slot < count[0])
    def _():
        shifted[0, :, HALF_T : HALF_T + samples] = x[0]
        shifted[1, :, HALF_T + 64 : HALF_T + 64 + samples] = x[0]
        for k in range(2):
            for lo, hi in column_tiles(samples):
                tp[k * half : (k + 1) * half, lo:hi] = jnp.dot(
                    xi[k * half : (k + 1) * half],
                    shifted[k, :, lo:hi],
                    preferred_element_type=F32,
                ).astype(BF16)
        weight = jnp.concatenate([w[0, EDGE : EDGE + rows]] * 2, axis=1)
        for first in range(0, samples // TILE, 2):
            tiles = (first, first + 1)
            for tile, noise in zip(tiles, noise_tiles(tp, m, dips, rows, tiles)):
                cols = slice(tile * TILE, (tile + 1) * TILE)
                center = x[0, EDGE : EDGE + rows, cols].astype(F32)
                o[0, EDGE : EDGE + rows, cols] = (center - weight * noise).astype(BF16)

    @pl.when(slot >= count[0])
    def _():
        o[...] = jnp.zeros_like(o)


def interior(count, x, w, xi, m, start, steps, out=None):
    slots, block, samples = x.shape
    dips = m.shape[0] * 2 // PAIR_K
    fetch = lambda i, n: (jnp.minimum(i + n[1], jnp.maximum(n[0] - 1, 0)), 0, 0)
    in_specs = [
        pl.BlockSpec((1, block, samples), fetch),
        pl.BlockSpec((1, block, 128), fetch),
        pl.BlockSpec(xi.shape, lambda i, n: (0, 0)),
        pl.BlockSpec(m.shape, lambda i, n: (0, 0)),
    ]
    args = [jnp.stack([count, jnp.int32(start)]), x, w, xi, m]
    aliases = {}
    if out is not None:
        in_specs.append(pl.BlockSpec(memory_space=pl.ANY))
        args.append(out)
        aliases = {5: 0}
    return pl.pallas_call(
        functools.partial(interior_kernel, dips),
        out_shape=jax.ShapeDtypeStruct(x.shape, BF16),
        grid_spec=pltpu.PrefetchScalarGridSpec(
            num_scalar_prefetch=1,
            grid=(steps,),
            in_specs=in_specs,
            out_specs=pl.BlockSpec((1, block, samples), lambda i, n: (i + n[1], 0, 0)),
            scratch_shapes=[
                pltpu.VMEM((2, block, samples + 128), BF16),
                pltpu.VMEM((xi.shape[0], samples + 128), BF16),
            ],
        ),
        input_output_aliases=aliases,
        compiler_params=params(),
        cost_estimate=cost(steps * 2_000_000_000, steps * 2**20),
        name="interior",
    )(*args)


def edge_kernel(dips, groups, count, xt, xb, halo, w, xe, m, _, o, shifted, tp, res, sems):
    g = pl.program_id(0)
    per = xt.shape[0]
    samples = xt.shape[2]
    rows = per * 2 * EDGE
    n_slices = halo.shape[0]
    half = xe.shape[0] // 2
    live = g * per < count[0]

    def copies(group):
        slots = pl.ds(group * per, per)
        return (
            pltpu.make_async_copy(
                res.at[group, :, pl.ds(0, EDGE)], o.at[slots, pl.ds(0, EDGE)], sems.at[group, 0]
            ),
            pltpu.make_async_copy(
                res.at[group, :, pl.ds(EDGE, EDGE)],
                o.at[slots, pl.ds(128 - EDGE, EDGE)],
                sems.at[group, 1],
            ),
        )

    @pl.when(g == 0)
    def _():
        shifted[...] = jnp.zeros_like(shifted)

    @pl.when(live)
    def _():
        for i in range(per):
            above = [halo[s, i * 32 : i * 32 + EDGE] for s in range(n_slices)]
            below = [halo[s, i * 32 + EDGE : i * 32 + 32] for s in range(n_slices)]
            above = jnp.concatenate(above, axis=1)
            below = jnp.concatenate(below, axis=1)
            for k in range(2):
                here = slice(HALF_T + 64 * k, HALF_T + 64 * k + samples)
                shifted[k, i, 0:16, here] = above
                shifted[k, i, 16:48, here] = xt[i]
                shifted[k, i, 48:80, here] = xb[i]
                shifted[k, i, 80:96, here] = below
                for lo, hi in column_tiles(samples):
                    part = jnp.dot(
                        xe[k * half : (k + 1) * half],
                        shifted[k, i, :, lo:hi],
                        preferred_element_type=F32,
                    ).astype(BF16)
                    for c in range(dips // 2):
                        at = (k * dips // 2 + c) * rows + i * 32
                        tp[at : at + 32, lo:hi] = part[c * 32 : c * 32 + 32]
        for tile in range(samples // TILE):
            cols = slice(tile * TILE, (tile + 1) * TILE)
            [noise] = noise_tiles(tp, m, dips, rows, (tile,))
            for i in range(per):
                keep = g * per + i < count[0]
                top = noise[i * 32 : i * 32 + 16]
                bottom = noise[i * 32 + 16 : i * 32 + 32]
                wt = jnp.concatenate([w[i, :EDGE]] * 2, axis=1)
                wb = jnp.concatenate([w[i, 128 - EDGE :]] * 2, axis=1)
                top = xt[i, :EDGE, cols].astype(F32) - wt * top
                bottom = xb[i, EDGE:, cols].astype(F32) - wb * bottom
                res[g, i, :EDGE, cols] = jnp.where(keep, top, 0.0).astype(BF16)
                res[g, i, EDGE:, cols] = jnp.where(keep, bottom, 0.0).astype(BF16)
        for copy in copies(g):
            copy.start()

    @pl.when(g == groups - 1)
    def _():
        for group in range(groups):

            @pl.when(group * per < count[0])
            def _():
                for copy in copies(group):
                    copy.wait()


def edges(count, x, halo, w, xe, m, out, per=6):
    slots, block, samples = x.shape
    dips = m.shape[0] * 2 // PAIR_K
    groups = slots // per
    last = lambda g, n: jnp.minimum(g, jnp.maximum(n[0] - 1, 0) // per)
    return pl.pallas_call(
        functools.partial(edge_kernel, dips, groups),
        out_shape=jax.ShapeDtypeStruct(x.shape, BF16),
        grid_spec=pltpu.PrefetchScalarGridSpec(
            num_scalar_prefetch=1,
            grid=(groups,),
            in_specs=[
                pl.BlockSpec((per, 32, samples), lambda g, n: (last(g, n), 0, 0)),
                pl.BlockSpec((per, 32, samples), lambda g, n: (last(g, n), 3, 0)),
                pl.BlockSpec((halo.shape[0], per * 32, 128), lambda g, n: (0, last(g, n), 0)),
                pl.BlockSpec((per, block, 128), lambda g, n: (last(g, n), 0, 0)),
                pl.BlockSpec(xe.shape, lambda g, n: (0, 0)),
                pl.BlockSpec(m.shape, lambda g, n: (0, 0)),
                pl.BlockSpec(memory_space=pl.ANY),
            ],
            out_specs=pl.BlockSpec(memory_space=pl.ANY),
            scratch_shapes=[
                pltpu.VMEM((2, per, 96, samples + 128), BF16),
                pltpu.VMEM((dips * per * 32, samples + 128), BF16),
                pltpu.VMEM((groups, per, 32, samples), BF16),
                pltpu.SemaphoreType.DMA((groups, 2)),
            ],
        ),
        input_output_aliases={7: 0},
        compiler_params=params(),
        cost_estimate=cost(8_000_000_000, 2**23),
        name="edges",
    )(count.reshape(1), x, x, halo, w, xe, m, out)


def payload_kernel(per_line, count, dest, offset, xt, xb, o):
    slots = xt.shape[0]
    slot = lax.broadcasted_iota(jnp.int32, (1, slots), 1)
    place = jnp.where(slot < count[0, 0], dest[...] * per_line + offset[...], -2)
    place = jnp.broadcast_to(place.astype(F32), (EDGE, slots)).astype(BF16)
    for s in range(o.shape[0]):
        cols = slice(s * 128, (s + 1) * 128)
        for i in range(slots):
            o[s, i * 32 : i * 32 + EDGE] = xt[i, :, cols]
            o[s, i * 32 + EDGE : i * 32 + 32] = xb[i, :, cols]
        o[s, slots * 32 :, 0:slots] = place


def payload(block_count, slot_dest, slot_offset, x, steps=4):
    slots, block, samples = x.shape
    slices = samples // 128
    per = slices // steps
    return pl.pallas_call(
        functools.partial(payload_kernel, slots // 2),
        out_shape=jax.ShapeDtypeStruct((slices, slots * 32 + EDGE, 128), BF16),
        grid=(steps,),
        in_specs=[
            pl.BlockSpec(memory_space=pltpu.SMEM),
            pl.BlockSpec((1, slots), lambda i: (0, 0)),
            pl.BlockSpec((1, slots), lambda i: (0, 0)),
            pl.BlockSpec((slots, EDGE, per * 128), lambda i: (0, 0, i)),
            pl.BlockSpec((slots, EDGE, per * 128), lambda i: (0, block // EDGE - 1, i)),
        ],
        out_specs=pl.BlockSpec((per, slots * 32 + EDGE, 128), lambda i: (i, 0, 0)),
        compiler_params=params(16 * 2**20),
        cost_estimate=cost(0, 2**22),
        name="payload",
    )(block_count, slot_dest, slot_offset, x, x)


def permute_kernel(slots, x, o, places, table, where, sem):
    sources = places.shape[0]
    stride = slots * 32 + EDGE
    for s in range(sources):
        row = x[s * stride + slots * 32 : (s + 1) * stride]
        places[s : s + 1] = row.astype(F32)[:1].astype(jnp.int32)
    copy = pltpu.make_async_copy(places, table, sem)
    copy.start()
    copy.wait()
    total = sources * (slots // 2)
    where[0] = -1
    where[total + 1] = -1

    def fill(s, _):
        for i in range(slots):
            p = table[s, i]
            where[jnp.where(p < 0, total + 2, p + 1)] = s * stride + i * 32
        return 0

    lax.fori_loop(0, sources, fill, 0)

    def move(s, _):
        for i in range(slots):
            p = jnp.maximum(table[s, i], 0)
            a = where[p]
            b = where[p + 2]
            above = x[pl.ds(pl.multiple_of(jnp.maximum(a, 0) + EDGE, EDGE), EDGE)]
            below = x[pl.ds(pl.multiple_of(jnp.maximum(b, 0), EDGE), EDGE)]
            o[s, i * 32 : i * 32 + EDGE] = jnp.where(a >= 0, above, jnp.zeros_like(above))
            o[s, i * 32 + EDGE : i * 32 + 32] = jnp.where(b >= 0, below, jnp.zeros_like(below))
        return 0

    lax.fori_loop(0, sources, move, 0)


def permute(x, slots):
    sources, rows, width = x.shape
    total = sources * (slots // 2)
    return pl.pallas_call(
        functools.partial(permute_kernel, slots),
        out_shape=jax.ShapeDtypeStruct((sources, slots * 32, width), BF16),
        in_specs=[pl.BlockSpec(memory_space=pltpu.VMEM)],
        out_specs=pl.BlockSpec(memory_space=pltpu.VMEM),
        scratch_shapes=[
            pltpu.VMEM((sources, 128), jnp.int32),
            pltpu.SMEM((sources, 128), jnp.int32),
            pltpu.SMEM((total + 3,), jnp.int32),
            pltpu.SemaphoreType.DMA,
        ],
        compiler_params=pltpu.CompilerParams(vmem_limit_bytes=16 * 2**20),
        cost_estimate=cost(0, 2**23),
        name="permute",
    )(x.reshape(sources * rows, width))


def shards(
    shot_traces, slot_dest, slot_offset, block_count, amp_index, amp_table, dip_trace, dip_time
):
    x = shot_traces[0]
    slots, block, samples = x.shape
    count = block_count[0, 0]

    ends = payload(block_count, slot_dest, slot_offset, x)
    ends = lax.all_to_all(ends, "rline", split_axis=0, concat_axis=0, tiled=True)

    amps = lax.all_gather(amp_table, "shot", axis=0, tiled=True)
    table_hit = amp_index[0][:, :, None] == jnp.arange(amps.shape[0], dtype=jnp.int32)
    weight = jnp.sum(jnp.where(table_hit, amps, F32(0.0)), axis=2)
    weight = jnp.broadcast_to(weight[:, :, None], (slots, block, 128))
    m, xi, xe = matrices(dip_trace, dip_time, block - 2 * EDGE)

    out = interior(count, x, weight, xi, m, 0, FIRST)
    moved = permute(ends, slots)
    halo = lax.all_to_all(moved, "rline", split_axis=0, concat_axis=0, tiled=True)
    out = interior(count, x, weight, xi, m, FIRST, slots - FIRST, out)
    out = edges(count, x, halo, weight, xe, m, out)
    return out[None]


def solution(mesh):
    in_specs = (
        P("shot", "rline", None, None),
        P("shot", "rline"),
        P("shot", "rline"),
        P("shot", "rline"),
        P("shot", "rline", None),
        P("shot"),
        P(),
        P(),
    )
    out_specs = P("shot", "rline", None, None)
    return jax.shard_map(shards, mesh=mesh, in_specs=in_specs, out_specs=out_specs, check_vma=False)
```

```python
import functools

import jax
import jax.numpy as jnp
from jax import lax
from jax.experimental import pallas as pl
from jax.experimental.pallas import tpu as pltpu
from jax.sharding import PartitionSpec as P

BF16 = jnp.bfloat16
F32 = jnp.float32
EDGE = 16
TILE = 256
HALF_T = 32
PAIR_K = 640
VMEM_LIMIT = 56 * 2**20
EDGE_VMEM = 52 * 2**20
FIRST = 6


def params(limit=VMEM_LIMIT):
    return pltpu.CompilerParams(dimension_semantics=("arbitrary",), vmem_limit_bytes=limit)


def cost(flops, bytes_accessed):
    return pl.CostEstimate(flops=flops, bytes_accessed=bytes_accessed, transcendentals=0)


def dip_order(dips):
    return list(range(0, dips, 2)) + list(range(1, dips, 2))


def matrices_kernel(taps_x, taps_t, m, xi, xe):
    dips = taps_x.shape[0]
    row = lax.broadcasted_iota(jnp.int32, (TILE, TILE), 0)
    col = lax.broadcasted_iota(jnp.int32, (TILE, TILE), 1)
    for c in range(dips):
        base = jnp.broadcast_to(taps_t[c : c + 1], (TILE, TILE))
        band = pltpu.roll(base, 0, 1, stride=1, stride_axis=0)
        at = c * (PAIR_K // 2)
        m[at : at + TILE] = jnp.where(col <= row, band, 0.0).astype(BF16)
        m[at + TILE : at + PAIR_K // 2] = jnp.where(col > row, band, 0.0)[:64].astype(BF16)
    rows = xi.shape[0] // dips
    for i, c in enumerate(dip_order(dips)):
        base = jnp.broadcast_to(taps_x[c : c + 1], (rows, 128))
        band = pltpu.roll(base, 0, 1, stride=1, stride_axis=0)
        xi[i * rows : (i + 1) * rows] = band.astype(BF16)
        xe[i * 32 : i * 32 + 16] = band[:16, :96].astype(BF16)
        xe[i * 32 + 16 : i * 32 + 32] = band[48:64, :96].astype(BF16)


def matrices(dip_trace, dip_time, rows):
    dips, taps = dip_time.shape
    taps_x = jnp.pad(dip_trace.astype(F32), ((0, 0), (0, 128 - dip_trace.shape[1])))
    taps_t = dip_time.astype(F32)
    gap = jnp.zeros((dips, TILE - taps), F32)
    taps_t = jnp.concatenate([taps_t[:, :1], gap, taps_t[:, :0:-1]], axis=1)
    return pl.pallas_call(
        matrices_kernel,
        out_shape=(
            jax.ShapeDtypeStruct((dips * PAIR_K // 2, TILE), BF16),
            jax.ShapeDtypeStruct((dips * rows, 128), BF16),
            jax.ShapeDtypeStruct((dips * 32, 96), BF16),
        ),
        compiler_params=pltpu.CompilerParams(vmem_limit_bytes=16 * 2**20),
        cost_estimate=cost(0, 2**21),
        name="matrices",
    )(taps_x, taps_t)


def time_lhs(tp, dips, rows, tile):
    base = tile * TILE
    low = lax.broadcasted_iota(jnp.int32, (rows, 128), 1) < 64
    parts = []
    for pair in range(dips // 2):
        even = pl.ds(pair * rows, rows)
        odd = pl.ds((dips // 2 + pair) * rows, rows)
        parts.append(tp[even, base : base + 256])
        parts.append(jnp.where(low, tp[even, base + 256 : base + 384], tp[odd, base : base + 128]))
        parts.append(tp[odd, base + 128 : base + 384])
    return jnp.concatenate(parts, axis=1)


def noise_tiles(tp, m, dips, rows, tiles):
    lhs = jnp.concatenate([time_lhs(tp, dips, rows, tile) for tile in tiles], axis=0)
    noise = jnp.dot(lhs, m[...], preferred_element_type=F32)
    return [noise[k * rows : (k + 1) * rows] for k in range(len(tiles))]


def column_tiles(samples):
    return [(lo, min(lo + TILE, samples + 128)) for lo in range(0, samples + 128, TILE)]


def interior_kernel(dips, count, x, w, xi, m, *refs):
    o, shifted, tp = refs[-3:]
    rows = x.shape[1] - 2 * EDGE
    samples = x.shape[2]
    half = dips // 2 * rows
    slot = pl.program_id(0) + count[1]

    @pl.when(pl.program_id(0) == 0)
    def _():
        shifted[...] = jnp.zeros_like(shifted)

    @pl.when(slot < count[0])
    def _():
        shifted[0, :, HALF_T : HALF_T + samples] = x[0]
        shifted[1, :, HALF_T + 64 : HALF_T + 64 + samples] = x[0]
        for k in range(2):
            for lo, hi in column_tiles(samples):
                tp[k * half : (k + 1) * half, lo:hi] = jnp.dot(
                    xi[k * half : (k + 1) * half],
                    shifted[k, :, lo:hi],
                    preferred_element_type=F32,
                ).astype(BF16)
        weight = jnp.concatenate([w[0, EDGE : EDGE + rows]] * 2, axis=1)
        for first in range(0, samples // TILE, 2):
            tiles = (first, first + 1)
            for tile, noise in zip(tiles, noise_tiles(tp, m, dips, rows, tiles)):
                cols = slice(tile * TILE, (tile + 1) * TILE)
                center = x[0, EDGE : EDGE + rows, cols].astype(F32)
                o[0, EDGE : EDGE + rows, cols] = (center - weight * noise).astype(BF16)

    @pl.when(slot >= count[0])
    def _():
        o[...] = jnp.zeros_like(o)


def interior(count, x, w, xi, m, start, steps, out=None):
    slots, block, samples = x.shape
    dips = m.shape[0] * 2 // PAIR_K
    fetch = lambda i, n: (jnp.minimum(i + n[1], jnp.maximum(n[0] - 1, 0)), 0, 0)
    in_specs = [
        pl.BlockSpec((1, block, samples), fetch),
        pl.BlockSpec((1, block, 128), fetch),
        pl.BlockSpec(xi.shape, lambda i, n: (0, 0)),
        pl.BlockSpec(m.shape, lambda i, n: (0, 0)),
    ]
    args = [jnp.stack([count, jnp.int32(start)]), x, w, xi, m]
    aliases = {}
    if out is not None:
        in_specs.append(pl.BlockSpec(memory_space=pl.ANY))
        args.append(out)
        aliases = {5: 0}
    return pl.pallas_call(
        functools.partial(interior_kernel, dips),
        out_shape=jax.ShapeDtypeStruct(x.shape, BF16),
        grid_spec=pltpu.PrefetchScalarGridSpec(
            num_scalar_prefetch=1,
            grid=(steps,),
            in_specs=in_specs,
            out_specs=pl.BlockSpec((1, block, samples), lambda i, n: (i + n[1], 0, 0)),
            scratch_shapes=[
                pltpu.VMEM((2, block, samples + 128), BF16),
                pltpu.VMEM((xi.shape[0], samples + 128), BF16),
            ],
        ),
        input_output_aliases=aliases,
        compiler_params=params(),
        cost_estimate=cost(steps * 2_000_000_000, steps * 2**20),
        name="interior",
    )(*args)


def edge_kernel(dips, groups, count, xt, xb, halo, w, xe, m, _, o, shifted, tp, res, sems):
    g = pl.program_id(0)
    per = xt.shape[0]
    samples = xt.shape[2]
    rows = per * 2 * EDGE
    n_slices = halo.shape[0]
    half = xe.shape[0] // 2
    live = g * per < count[0]

    def copies(group):
        slots = pl.ds(group * per, per)
        return (
            pltpu.make_async_copy(
                res.at[group, :, pl.ds(0, EDGE)], o.at[slots, pl.ds(0, EDGE)], sems.at[group, 0]
            ),
            pltpu.make_async_copy(
                res.at[group, :, pl.ds(EDGE, EDGE)],
                o.at[slots, pl.ds(128 - EDGE, EDGE)],
                sems.at[group, 1],
            ),
        )

    @pl.when(g == 0)
    def _():
        shifted[...] = jnp.zeros_like(shifted)

    @pl.when(live)
    def _():
        for i in range(per):
            above = [halo[s, i * 32 : i * 32 + EDGE] for s in range(n_slices)]
            below = [halo[s, i * 32 + EDGE : i * 32 + 32] for s in range(n_slices)]
            above = jnp.concatenate(above, axis=1)
            below = jnp.concatenate(below, axis=1)
            for k in range(2):
                here = slice(HALF_T + 64 * k, HALF_T + 64 * k + samples)
                shifted[k, i, 0:16, here] = above
                shifted[k, i, 16:48, here] = xt[i]
                shifted[k, i, 48:80, here] = xb[i]
                shifted[k, i, 80:96, here] = below
                for lo, hi in column_tiles(samples):
                    part = jnp.dot(
                        xe[k * half : (k + 1) * half],
                        shifted[k, i, :, lo:hi],
                        preferred_element_type=F32,
                    ).astype(BF16)
                    for c in range(dips // 2):
                        at = (k * dips // 2 + c) * rows + i * 32
                        tp[at : at + 32, lo:hi] = part[c * 32 : c * 32 + 32]
        for tile in range(samples // TILE):
            cols = slice(tile * TILE, (tile + 1) * TILE)
            [noise] = noise_tiles(tp, m, dips, rows, (tile,))
            for i in range(per):
                keep = g * per + i < count[0]
                top = noise[i * 32 : i * 32 + 16]
                bottom = noise[i * 32 + 16 : i * 32 + 32]
                wt = jnp.concatenate([w[i, :EDGE]] * 2, axis=1)
                wb = jnp.concatenate([w[i, 128 - EDGE :]] * 2, axis=1)
                top = xt[i, :EDGE, cols].astype(F32) - wt * top
                bottom = xb[i, EDGE:, cols].astype(F32) - wb * bottom
                res[g, i, :EDGE, cols] = jnp.where(keep, top, 0.0).astype(BF16)
                res[g, i, EDGE:, cols] = jnp.where(keep, bottom, 0.0).astype(BF16)
        for copy in copies(g):
            copy.start()

    @pl.when(g == groups - 1)
    def _():
        for group in range(groups):

            @pl.when(group * per < count[0])
            def _():
                for copy in copies(group):
                    copy.wait()


def edges(count, x, halo, w, xe, m, out, per=6):
    slots, block, samples = x.shape
    dips = m.shape[0] * 2 // PAIR_K
    groups = slots // per
    last = lambda g, n: jnp.minimum(g, jnp.maximum(n[0] - 1, 0) // per)
    return pl.pallas_call(
        functools.partial(edge_kernel, dips, groups),
        out_shape=jax.ShapeDtypeStruct(x.shape, BF16),
        grid_spec=pltpu.PrefetchScalarGridSpec(
            num_scalar_prefetch=1,
            grid=(groups,),
            in_specs=[
                pl.BlockSpec((per, 32, samples), lambda g, n: (last(g, n), 0, 0)),
                pl.BlockSpec((per, 32, samples), lambda g, n: (last(g, n), 3, 0)),
                pl.BlockSpec((halo.shape[0], per * 32, 128), lambda g, n: (0, last(g, n), 0)),
                pl.BlockSpec((per, block, 128), lambda g, n: (last(g, n), 0, 0)),
                pl.BlockSpec(xe.shape, lambda g, n: (0, 0)),
                pl.BlockSpec(m.shape, lambda g, n: (0, 0)),
                pl.BlockSpec(memory_space=pl.ANY),
            ],
            out_specs=pl.BlockSpec(memory_space=pl.ANY),
            scratch_shapes=[
                pltpu.VMEM((2, per, 96, samples + 128), BF16),
                pltpu.VMEM((dips * per * 32, samples + 128), BF16),
                pltpu.VMEM((groups, per, 32, samples), BF16),
                pltpu.SemaphoreType.DMA((groups, 2)),
            ],
        ),
        input_output_aliases={7: 0},
        compiler_params=params(EDGE_VMEM),
        cost_estimate=cost(8_000_000_000, 2**23),
        name="edges",
    )(count.reshape(1), x, x, halo, w, xe, m, out)


def payload_kernel(per_line, count, dest, offset, xt, xb, o):
    slots = xt.shape[0]
    slot = lax.broadcasted_iota(jnp.int32, (1, slots), 1)
    place = jnp.where(slot < count[0, 0], dest[...] * per_line + offset[...], -2)
    place = jnp.broadcast_to(place.astype(F32), (EDGE, slots)).astype(BF16)
    for s in range(o.shape[0]):
        cols = slice(s * 128, (s + 1) * 128)
        for i in range(slots):
            o[s, i * 32 : i * 32 + EDGE] = xt[i, :, cols]
            o[s, i * 32 + EDGE : i * 32 + 32] = xb[i, :, cols]
        o[s, slots * 32 :, 0:slots] = place


def payload(block_count, slot_dest, slot_offset, x, steps=4):
    slots, block, samples = x.shape
    slices = samples // 128
    per = slices // steps
    return pl.pallas_call(
        functools.partial(payload_kernel, slots // 2),
        out_shape=jax.ShapeDtypeStruct((slices, slots * 32 + EDGE, 128), BF16),
        grid=(steps,),
        in_specs=[
            pl.BlockSpec(memory_space=pltpu.SMEM),
            pl.BlockSpec((1, slots), lambda i: (0, 0)),
            pl.BlockSpec((1, slots), lambda i: (0, 0)),
            pl.BlockSpec((slots, EDGE, per * 128), lambda i: (0, 0, i)),
            pl.BlockSpec((slots, EDGE, per * 128), lambda i: (0, block // EDGE - 1, i)),
        ],
        out_specs=pl.BlockSpec((per, slots * 32 + EDGE, 128), lambda i: (i, 0, 0)),
        compiler_params=params(),
        cost_estimate=cost(0, 2**22),
        name="payload",
    )(block_count, slot_dest, slot_offset, x, x)


def permute_kernel(slots, x, o, places, table, where, sem):
    sources = places.shape[0]
    stride = slots * 32 + EDGE
    for s in range(sources):
        row = x[s * stride + slots * 32 : (s + 1) * stride]
        places[s : s + 1] = row.astype(F32)[:1].astype(jnp.int32)
    copy = pltpu.make_async_copy(places, table, sem)
    copy.start()
    copy.wait()
    total = sources * (slots // 2)
    where[0] = -1
    where[total + 1] = -1

    def fill(s, _):
        for i in range(slots):
            p = table[s, i]
            where[jnp.where(p < 0, total + 2, p + 1)] = s * stride + i * 32
        return 0

    lax.fori_loop(0, sources, fill, 0)

    def move(s, _):
        for i in range(slots):
            p = jnp.maximum(table[s, i], 0)
            a = where[p]
            b = where[p + 2]
            above = x[pl.ds(pl.multiple_of(jnp.maximum(a, 0) + EDGE, EDGE), EDGE)]
            below = x[pl.ds(pl.multiple_of(jnp.maximum(b, 0), EDGE), EDGE)]
            o[s, i * 32 : i * 32 + EDGE] = jnp.where(a >= 0, above, jnp.zeros_like(above))
            o[s, i * 32 + EDGE : i * 32 + 32] = jnp.where(b >= 0, below, jnp.zeros_like(below))
        return 0

    lax.fori_loop(0, sources, move, 0)


def permute(x, slots):
    sources, rows, width = x.shape
    total = sources * (slots // 2)
    return pl.pallas_call(
        functools.partial(permute_kernel, slots),
        out_shape=jax.ShapeDtypeStruct((sources, slots * 32, width), BF16),
        in_specs=[pl.BlockSpec(memory_space=pltpu.VMEM)],
        out_specs=pl.BlockSpec(memory_space=pltpu.VMEM),
        scratch_shapes=[
            pltpu.VMEM((sources, 128), jnp.int32),
            pltpu.SMEM((sources, 128), jnp.int32),
            pltpu.SMEM((total + 3,), jnp.int32),
            pltpu.SemaphoreType.DMA,
        ],
        compiler_params=pltpu.CompilerParams(vmem_limit_bytes=16 * 2**20),
        cost_estimate=cost(0, 2**23),
        name="permute",
    )(x.reshape(sources * rows, width))


def shards(
    shot_traces, slot_dest, slot_offset, block_count, amp_index, amp_table, dip_trace, dip_time
):
    x = shot_traces[0]
    slots, block, samples = x.shape
    count = block_count[0, 0]

    ends = payload(block_count, slot_dest, slot_offset, x)
    ends = lax.all_to_all(ends, "rline", split_axis=0, concat_axis=0, tiled=True)

    amps = lax.all_gather(amp_table, "shot", axis=0, tiled=True)
    table_hit = amp_index[0][:, :, None] == jnp.arange(amps.shape[0], dtype=jnp.int32)
    weight = jnp.sum(jnp.where(table_hit, amps, F32(0.0)), axis=2)
    weight = jnp.broadcast_to(weight[:, :, None], (slots, block, 128))
    m, xi, xe = matrices(dip_trace, dip_time, block - 2 * EDGE)

    out = interior(count, x, weight, xi, m, 0, FIRST)
    ends, out = lax.optimization_barrier((ends, out))
    moved = permute(ends, slots)
    halo = lax.all_to_all(moved, "rline", split_axis=0, concat_axis=0, tiled=True)
    out = interior(count, x, weight, xi, m, FIRST, slots - FIRST, out)
    out = edges(count, x, halo, weight, xe, m, out)
    return out[None]


def solution(mesh):
    in_specs = (
        P("shot", "rline", None, None),
        P("shot", "rline"),
        P("shot", "rline"),
        P("shot", "rline"),
        P("shot", "rline", None),
        P("shot"),
        P(),
        P(),
    )
    out_specs = P("shot", "rline", None, None)
    return jax.shard_map(shards, mesh=mesh, in_specs=in_specs, out_specs=out_specs, check_vma=False)
```

```python
import functools

import jax
import jax.numpy as jnp
from jax import lax
from jax.experimental import pallas as pl
from jax.experimental.pallas import tpu as pltpu
from jax.sharding import PartitionSpec as P

BF16 = jnp.bfloat16
F32 = jnp.float32
EDGE = 16
TILE = 256
HALF_T = 32
PAIR_K = 640
VMEM_LIMIT = 56 * 2**20
EDGE_VMEM = 50 * 2**20
FIRST = 9
TABLE_ROWS = 256


def params(limit=VMEM_LIMIT):
    return pltpu.CompilerParams(dimension_semantics=("arbitrary",), vmem_limit_bytes=limit)


def cost(flops, bytes_accessed):
    return pl.CostEstimate(flops=flops, bytes_accessed=bytes_accessed, transcendentals=0)


def fill_time_bands(taps, m):
    row = lax.broadcasted_iota(jnp.int32, (TILE, TILE), 0)
    col = lax.broadcasted_iota(jnp.int32, (TILE, TILE), 1)
    for c in range(taps.shape[0]):
        base = jnp.broadcast_to(taps[c : c + 1], (TILE, TILE))
        band = pltpu.roll(base, 0, 1, stride=1, stride_axis=0)
        at = c * (PAIR_K // 2)
        m[at : at + TILE] = jnp.where(col <= row, band, 0.0).astype(BF16)
        m[at + TILE : at + PAIR_K // 2] = jnp.where(col > row, band, 0.0)[:64].astype(BF16)


def trace_bands(taps, rows):
    dips = taps.shape[0]
    for c in list(range(0, dips, 2)) + list(range(1, dips, 2)):
        base = jnp.broadcast_to(taps[c : c + 1], (rows, 128))
        yield pltpu.roll(base, 0, 1, stride=1, stride_axis=0).astype(BF16)


def spread_taps(dip_trace, dip_time):
    dips, taps = dip_time.shape
    taps_x = jnp.pad(dip_trace.astype(F32), ((0, 0), (0, 128 - dip_trace.shape[1])))
    taps_t = dip_time.astype(F32)
    gap = jnp.zeros((dips, TILE - taps), F32)
    return taps_x, jnp.concatenate([taps_t[:, :1], gap, taps_t[:, :0:-1]], axis=1)


def turned(x, by):
    return jnp.concatenate([x[:, x.shape[1] - by :], x[:, : x.shape[1] - by]], axis=1)


def time_lhs(tp, dips, rows, tile):
    samples = tp.shape[1]
    lane = lax.broadcasted_iota(jnp.int32, (rows, 128), 1)
    zero = jnp.zeros((rows, 128), BF16)
    first, last = tile == 0, tile == samples // TILE - 1
    at = [(tile * TILE + 128 * k) % samples for k in range(3)]
    parts = []
    for pair in range(dips // 2):
        even = [tp[pl.ds(pair * rows, rows), lo : lo + 128] for lo in at]
        odd = [tp[pl.ds((dips // 2 + pair) * rows, rows), lo : lo + 128] for lo in at]
        if first:
            even[0] = jnp.where(lane < HALF_T, zero, even[0])
            odd[0] = jnp.where(lane < HALF_T + 64, zero, odd[0])
        if last:
            even[2] = jnp.where(lane < HALF_T, even[2], zero)
            odd[2] = jnp.where(lane < HALF_T + 64, odd[2], zero)
        parts += [even[0], even[1], jnp.where(lane < 64, even[2], odd[0]), odd[1], odd[2]]
    return jnp.concatenate(parts, axis=1)


def noise_tiles(tp, m, dips, rows, tiles):
    lhs = jnp.concatenate([time_lhs(tp, dips, rows, tile) for tile in tiles], axis=0)
    noise = jnp.dot(lhs, m[...], preferred_element_type=F32)
    return [noise[k * rows : (k + 1) * rows] for k in range(len(tiles))]


def column_tiles(samples):
    return [(lo, lo + TILE) for lo in range(0, samples, TILE)]


def interior_kernel(start, count, x, w, taps_x, taps_t, *refs):
    o, shifted, tp, xi, m = refs[-5:]
    dips = taps_x.shape[0]
    rows = x.shape[1] - 2 * EDGE
    samples = x.shape[2]
    half = dips // 2 * rows
    slot = pl.program_id(0) + start

    @pl.when(pl.program_id(0) == 0)
    def _():
        fill_time_bands(taps_t, m)
        for i, band in enumerate(trace_bands(taps_x, rows)):
            xi[i * rows : (i + 1) * rows] = band

    @pl.when(slot < count[0])
    def _():
        for k in range(2):
            shifted[k] = turned(x[0], HALF_T + 64 * k)
        for k in range(2):
            for lo, hi in column_tiles(samples):
                tp[k * half : (k + 1) * half, lo:hi] = jnp.dot(
                    xi[k * half : (k + 1) * half],
                    shifted[k, :, lo:hi],
                    preferred_element_type=F32,
                ).astype(BF16)
        weight = jnp.concatenate([w[0, EDGE : EDGE + rows]] * 2, axis=1)
        for first in range(0, samples // TILE, 2):
            tiles = (first, first + 1)
            for tile, noise in zip(tiles, noise_tiles(tp, m, dips, rows, tiles)):
                cols = slice(tile * TILE, (tile + 1) * TILE)
                center = x[0, EDGE : EDGE + rows, cols].astype(F32)
                o[0, EDGE : EDGE + rows, cols] = (center - weight * noise).astype(BF16)

    @pl.when(slot >= count[0])
    def _():
        o[...] = jnp.zeros_like(o)


def interior(count, x, w, taps_x, taps_t, start, steps, out=None):
    slots, block, samples = x.shape
    dips = taps_x.shape[0]
    inner = dips * (block - 2 * EDGE)
    fetch = lambda i, n: (jnp.minimum(i + start, jnp.maximum(n[0] - 1, 0)), 0, 0)
    in_specs = [
        pl.BlockSpec((1, block, samples), fetch),
        pl.BlockSpec((1, block, 128), fetch),
        pl.BlockSpec(taps_x.shape, lambda i, n: (0, 0)),
        pl.BlockSpec(taps_t.shape, lambda i, n: (0, 0)),
    ]
    args = [count, x, w, taps_x, taps_t]
    aliases = {}
    if out is not None:
        in_specs.append(pl.BlockSpec(memory_space=pl.ANY))
        args.append(out)
        aliases = {5: 0}
    return pl.pallas_call(
        functools.partial(interior_kernel, start),
        out_shape=jax.ShapeDtypeStruct(x.shape, BF16),
        grid_spec=pltpu.PrefetchScalarGridSpec(
            num_scalar_prefetch=1,
            grid=(steps,),
            in_specs=in_specs,
            out_specs=pl.BlockSpec((1, block, samples), lambda i, n: (i + start, 0, 0)),
            scratch_shapes=[
                pltpu.VMEM((2, block, samples), BF16),
                pltpu.VMEM((inner, samples), BF16),
                pltpu.VMEM((inner, block), BF16),
                pltpu.VMEM((dips * PAIR_K // 2, TILE), BF16),
            ],
        ),
        input_output_aliases=aliases,
        compiler_params=params(),
        cost_estimate=cost(steps * 2_000_000_000, steps * 2**20),
        name="interior",
    )(*args)


def edge_kernel(
    groups, count, xt, xb, halo, w, taps_x, taps_t, _, o, shifted, tp, res, xe, m, sems
):
    dips = taps_x.shape[0]
    g = pl.program_id(0)
    per = xt.shape[0]
    samples = xt.shape[2]
    rows = per * 2 * EDGE
    n_slices = halo.shape[0]
    half = xe.shape[0] // 2
    live = g * per < count[0]

    def copies(group):
        slots = pl.ds(group * per, per)
        return (
            pltpu.make_async_copy(
                res.at[group, :, pl.ds(0, EDGE)], o.at[slots, pl.ds(0, EDGE)], sems.at[group, 0]
            ),
            pltpu.make_async_copy(
                res.at[group, :, pl.ds(EDGE, EDGE)],
                o.at[slots, pl.ds(128 - EDGE, EDGE)],
                sems.at[group, 1],
            ),
        )

    @pl.when(g == 0)
    def _():
        fill_time_bands(taps_t, m)
        for i, band in enumerate(trace_bands(taps_x, 64)):
            xe[i * 32 : i * 32 + 16] = band[:16, :96]
            xe[i * 32 + 16 : i * 32 + 32] = band[48:, :96]

    @pl.when(live)
    def _():
        for i in range(per):
            above = [halo[s, i * 32 : i * 32 + EDGE] for s in range(n_slices)]
            below = [halo[s, i * 32 + EDGE : i * 32 + 32] for s in range(n_slices)]
            above = jnp.concatenate(above, axis=1)
            below = jnp.concatenate(below, axis=1)
            for k in range(2):
                by = HALF_T + 64 * k
                shifted[k, i, 0:16] = turned(above, by)
                shifted[k, i, 16:48] = turned(xt[i], by)
                shifted[k, i, 48:80] = turned(xb[i], by)
                shifted[k, i, 80:96] = turned(below, by)
                for lo, hi in column_tiles(samples):
                    part = jnp.dot(
                        xe[k * half : (k + 1) * half],
                        shifted[k, i, :, lo:hi],
                        preferred_element_type=F32,
                    ).astype(BF16)
                    for c in range(dips // 2):
                        at = (k * dips // 2 + c) * rows + i * 32
                        tp[at : at + 32, lo:hi] = part[c * 32 : c * 32 + 32]
        for tile in range(samples // TILE):
            cols = slice(tile * TILE, (tile + 1) * TILE)
            [noise] = noise_tiles(tp, m, dips, rows, (tile,))
            for i in range(per):
                keep = g * per + i < count[0]
                top = noise[i * 32 : i * 32 + 16]
                bottom = noise[i * 32 + 16 : i * 32 + 32]
                wt = jnp.concatenate([w[i, :EDGE]] * 2, axis=1)
                wb = jnp.concatenate([w[i, 128 - EDGE :]] * 2, axis=1)
                top = xt[i, :EDGE, cols].astype(F32) - wt * top
                bottom = xb[i, EDGE:, cols].astype(F32) - wb * bottom
                res[g, i, :EDGE, cols] = jnp.where(keep, top, 0.0).astype(BF16)
                res[g, i, EDGE:, cols] = jnp.where(keep, bottom, 0.0).astype(BF16)
        for copy in copies(g):
            copy.start()

    @pl.when(g == groups - 1)
    def _():
        for group in range(groups):

            @pl.when(group * per < count[0])
            def _():
                for copy in copies(group):
                    copy.wait()


def edges(count, x, halo, w, taps_x, taps_t, out, per=6):
    slots, block, samples = x.shape
    dips = taps_x.shape[0]
    groups = slots // per
    last = lambda g, n: jnp.minimum(g, jnp.maximum(n[0] - 1, 0) // per)
    return pl.pallas_call(
        functools.partial(edge_kernel, groups),
        out_shape=jax.ShapeDtypeStruct(x.shape, BF16),
        grid_spec=pltpu.PrefetchScalarGridSpec(
            num_scalar_prefetch=1,
            grid=(groups,),
            in_specs=[
                pl.BlockSpec((per, 32, samples), lambda g, n: (last(g, n), 0, 0)),
                pl.BlockSpec((per, 32, samples), lambda g, n: (last(g, n), 3, 0)),
                pl.BlockSpec((halo.shape[0], per * 32, 128), lambda g, n: (0, last(g, n), 0)),
                pl.BlockSpec((per, block, 128), lambda g, n: (last(g, n), 0, 0)),
                pl.BlockSpec(taps_x.shape, lambda g, n: (0, 0)),
                pl.BlockSpec(taps_t.shape, lambda g, n: (0, 0)),
                pl.BlockSpec(memory_space=pl.ANY),
            ],
            out_specs=pl.BlockSpec(memory_space=pl.ANY),
            scratch_shapes=[
                pltpu.VMEM((2, per, 96, samples), BF16),
                pltpu.VMEM((dips * per * 32, samples), BF16),
                pltpu.VMEM((groups, per, 32, samples), BF16),
                pltpu.VMEM((dips * 32, 96), BF16),
                pltpu.VMEM((dips * PAIR_K // 2, TILE), BF16),
                pltpu.SemaphoreType.DMA((groups, 2)),
            ],
        ),
        input_output_aliases={7: 0},
        compiler_params=params(EDGE_VMEM),
        cost_estimate=cost(8_000_000_000, 2**23),
        name="edges",
    )(count, x, x, halo, w, taps_x, taps_t, out)


def payload_kernel(per_line, count, dest, offset, xt, xb, o):
    slots = xt.shape[0]
    slot = lax.broadcasted_iota(jnp.int32, (1, slots), 1)
    place = jnp.where(slot < count[0, 0], dest[...] * per_line + offset[...], -2)
    place = jnp.broadcast_to(place.astype(F32), (EDGE, slots)).astype(BF16)
    for s in range(o.shape[0]):
        cols = slice(s * 128, (s + 1) * 128)
        for i in range(slots):
            o[s, i * 32 : i * 32 + EDGE] = xt[i, :, cols]
            o[s, i * 32 + EDGE : i * 32 + 32] = xb[i, :, cols]
        o[s, slots * 32 :, 0:slots] = place


def payload(block_count, slot_dest, slot_offset, x, steps=4):
    slots, block, samples = x.shape
    slices = samples // 128
    per = slices // steps
    return pl.pallas_call(
        functools.partial(payload_kernel, slots // 2),
        out_shape=jax.ShapeDtypeStruct((slices, slots * 32 + EDGE, 128), BF16),
        grid=(steps,),
        in_specs=[
            pl.BlockSpec(memory_space=pltpu.SMEM),
            pl.BlockSpec((1, slots), lambda i: (0, 0)),
            pl.BlockSpec((1, slots), lambda i: (0, 0)),
            pl.BlockSpec((slots, EDGE, per * 128), lambda i: (0, 0, i)),
            pl.BlockSpec((slots, EDGE, per * 128), lambda i: (0, block // EDGE - 1, i)),
        ],
        out_specs=pl.BlockSpec((per, slots * 32 + EDGE, 128), lambda i: (i, 0, 0)),
        compiler_params=params(),
        cost_estimate=cost(0, 2**22),
        name="payload",
    )(block_count, slot_dest, slot_offset, x, x)


def permute_kernel(slots, x, o, places, table, where, sem):
    sources = places.shape[0]
    stride = slots * 32 + EDGE
    for s in range(sources):
        row = x[s * stride + slots * 32 : (s + 1) * stride]
        places[s : s + 1] = row.astype(F32)[:1].astype(jnp.int32)
    copy = pltpu.make_async_copy(places, table, sem)
    copy.start()
    copy.wait()
    total = sources * (slots // 2)
    where[0] = -1
    where[total + 1] = -1

    def fill(s, _):
        for i in range(slots):
            p = table[s, i]
            where[jnp.where(p < 0, total + 2, p + 1)] = s * stride + i * 32
        return 0

    lax.fori_loop(0, sources, fill, 0)

    def move(s, _):
        for i in range(slots):
            p = jnp.maximum(table[s, i], 0)
            a = where[p]
            b = where[p + 2]
            above = x[pl.ds(pl.multiple_of(jnp.maximum(a, 0) + EDGE, EDGE), EDGE)]
            below = x[pl.ds(pl.multiple_of(jnp.maximum(b, 0), EDGE), EDGE)]
            o[s, i * 32 : i * 32 + EDGE] = jnp.where(a >= 0, above, jnp.zeros_like(above))
            o[s, i * 32 + EDGE : i * 32 + 32] = jnp.where(b >= 0, below, jnp.zeros_like(below))
        return 0

    lax.fori_loop(0, sources, move, 0)


def permute(x, slots):
    sources, rows, width = x.shape
    total = sources * (slots // 2)
    return pl.pallas_call(
        functools.partial(permute_kernel, slots),
        out_shape=jax.ShapeDtypeStruct((sources, slots * 32, width), BF16),
        in_specs=[pl.BlockSpec(memory_space=pltpu.VMEM)],
        out_specs=pl.BlockSpec(memory_space=pltpu.VMEM),
        scratch_shapes=[
            pltpu.VMEM((sources, 128), jnp.int32),
            pltpu.SMEM((sources, 128), jnp.int32),
            pltpu.SMEM((total + 3,), jnp.int32),
            pltpu.SemaphoreType.DMA,
        ],
        compiler_params=pltpu.CompilerParams(vmem_limit_bytes=16 * 2**20),
        cost_estimate=cost(0, 2**23),
        name="permute",
    )(x.reshape(sources * rows, width))


def shards(
    shot_traces, slot_dest, slot_offset, block_count, amp_index, amp_table, dip_trace, dip_time
):
    x = shot_traces[0]
    slots, block, samples = x.shape
    count = block_count.reshape(1)

    ends = payload(block_count, slot_dest, slot_offset, x)
    ends = lax.all_to_all(ends, "rline", split_axis=0, concat_axis=0, tiled=True)

    wide = jnp.broadcast_to(amp_table, (TABLE_ROWS, amp_table.shape[0]))
    wide = lax.all_gather(lax.optimization_barrier(wide), "shot", axis=0, tiled=False)
    amps = lax.optimization_barrier(wide)[:, 0].reshape(-1)
    table_hit = amp_index[0][:, :, None] == jnp.arange(amps.shape[0], dtype=jnp.int32)
    weight = jnp.sum(jnp.where(table_hit, amps, F32(0.0)), axis=2)
    weight = jnp.broadcast_to(weight[:, :, None], (slots, block, 128))
    taps_x, taps_t = spread_taps(dip_trace, dip_time)

    out = interior(count, x, weight, taps_x, taps_t, 0, FIRST)
    ends, out = lax.optimization_barrier((ends, out))
    moved = permute(ends, slots)
    halo = lax.all_to_all(moved, "rline", split_axis=0, concat_axis=0, tiled=True)
    out = interior(count, x, weight, taps_x, taps_t, FIRST, slots - FIRST, out)
    out = edges(count, x, halo, weight, taps_x, taps_t, out)
    return out[None]


def solution(mesh):
    in_specs = (
        P("shot", "rline", None, None),
        P("shot", "rline"),
        P("shot", "rline"),
        P("shot", "rline"),
        P("shot", "rline", None),
        P("shot"),
        P(),
        P(),
    )
    out_specs = P("shot", "rline", None, None)
    return jax.shard_map(shards, mesh=mesh, in_specs=in_specs, out_specs=out_specs, check_vma=False)
```

```python
import functools

import jax
import jax.numpy as jnp
from jax import lax
from jax.experimental import pallas as pl
from jax.experimental.pallas import tpu as pltpu
from jax.sharding import PartitionSpec as P

BF16 = jnp.bfloat16
F32 = jnp.float32
EDGE = 16
TILE = 256
HALF_T = 32
PAIR_K = 640
VMEM_LIMIT = 56 * 2**20
EDGE_VMEM = 50 * 2**20
FIRST = 6


def params(limit=VMEM_LIMIT):
    return pltpu.CompilerParams(dimension_semantics=("arbitrary",), vmem_limit_bytes=limit)


def cost(flops, bytes_accessed):
    return pl.CostEstimate(flops=flops, bytes_accessed=bytes_accessed, transcendentals=0)


def fill_time_bands(taps, m):
    row = lax.broadcasted_iota(jnp.int32, (TILE, TILE), 0)
    col = lax.broadcasted_iota(jnp.int32, (TILE, TILE), 1)
    for c in range(taps.shape[0]):
        base = jnp.broadcast_to(taps[c : c + 1], (TILE, TILE))
        band = pltpu.roll(base, 0, 1, stride=1, stride_axis=0)
        at = c * (PAIR_K // 2)
        m[at : at + TILE] = jnp.where(col <= row, band, 0.0).astype(BF16)
        m[at + TILE : at + PAIR_K // 2] = jnp.where(col > row, band, 0.0)[:64].astype(BF16)


def trace_bands(taps, rows):
    dips = taps.shape[0]
    for c in list(range(0, dips, 2)) + list(range(1, dips, 2)):
        base = jnp.broadcast_to(taps[c : c + 1], (rows, 128))
        yield pltpu.roll(base, 0, 1, stride=1, stride_axis=0).astype(BF16)


def spread_taps(dip_trace, dip_time):
    dips, taps = dip_time.shape
    taps_x = jnp.pad(dip_trace.astype(F32), ((0, 0), (0, 128 - dip_trace.shape[1])))
    taps_t = dip_time.astype(F32)
    gap = jnp.zeros((dips, TILE - taps), F32)
    return taps_x, jnp.concatenate([taps_t[:, :1], gap, taps_t[:, :0:-1]], axis=1)


def turned(x, by):
    return jnp.concatenate([x[:, x.shape[1] - by :], x[:, : x.shape[1] - by]], axis=1)


def time_lhs(tp, dips, rows, tile):
    samples = tp.shape[1]
    lane = lax.broadcasted_iota(jnp.int32, (rows, 128), 1)
    zero = jnp.zeros((rows, 128), BF16)
    first, last = tile == 0, tile == samples // TILE - 1
    at = [(tile * TILE + 128 * k) % samples for k in range(3)]
    parts = []
    for pair in range(dips // 2):
        even = [tp[pl.ds(pair * rows, rows), lo : lo + 128] for lo in at]
        odd = [tp[pl.ds((dips // 2 + pair) * rows, rows), lo : lo + 128] for lo in at]
        if first:
            even[0] = jnp.where(lane < HALF_T, zero, even[0])
            odd[0] = jnp.where(lane < HALF_T + 64, zero, odd[0])
        if last:
            even[2] = jnp.where(lane < HALF_T, even[2], zero)
            odd[2] = jnp.where(lane < HALF_T + 64, odd[2], zero)
        parts += [even[0], even[1], jnp.where(lane < 64, even[2], odd[0]), odd[1], odd[2]]
    return jnp.concatenate(parts, axis=1)


def noise_tiles(tp, m, dips, rows, tiles):
    lhs = jnp.concatenate([time_lhs(tp, dips, rows, tile) for tile in tiles], axis=0)
    noise = jnp.dot(lhs, m[...], preferred_element_type=F32)
    return [noise[k * rows : (k + 1) * rows] for k in range(len(tiles))]


def column_tiles(samples):
    return [(lo, lo + TILE) for lo in range(0, samples, TILE)]


def interior_kernel(start, count, x, w, taps_x, taps_t, *refs):
    o, shifted, tp, xi, m = refs[-5:]
    dips = taps_x.shape[0]
    rows = x.shape[1] - 2 * EDGE
    samples = x.shape[2]
    half = dips // 2 * rows
    slot = pl.program_id(0) + start

    @pl.when(pl.program_id(0) == 0)
    def _():
        fill_time_bands(taps_t, m)
        for i, band in enumerate(trace_bands(taps_x, rows)):
            xi[i * rows : (i + 1) * rows] = band

    @pl.when(slot < count[0])
    def _():
        for k in range(2):
            shifted[k] = turned(x[0], HALF_T + 64 * k)
        for k in range(2):
            for lo, hi in column_tiles(samples):
                tp[k * half : (k + 1) * half, lo:hi] = jnp.dot(
                    xi[k * half : (k + 1) * half],
                    shifted[k, :, lo:hi],
                    preferred_element_type=F32,
                ).astype(BF16)
        weight = jnp.concatenate([w[0, EDGE : EDGE + rows]] * 2, axis=1)
        for first in range(0, samples // TILE, 2):
            tiles = (first, first + 1)
            for tile, noise in zip(tiles, noise_tiles(tp, m, dips, rows, tiles)):
                cols = slice(tile * TILE, (tile + 1) * TILE)
                center = x[0, EDGE : EDGE + rows, cols].astype(F32)
                o[0, EDGE : EDGE + rows, cols] = (center - weight * noise).astype(BF16)

    @pl.when(slot >= count[0])
    def _():
        o[...] = jnp.zeros_like(o)


def interior(count, x, w, taps_x, taps_t, start, steps, out=None):
    slots, block, samples = x.shape
    dips = taps_x.shape[0]
    inner = dips * (block - 2 * EDGE)
    fetch = lambda i, n: (jnp.minimum(i + start, jnp.maximum(n[0] - 1, 0)), 0, 0)
    in_specs = [
        pl.BlockSpec((1, block, samples), fetch),
        pl.BlockSpec((1, block, 128), fetch),
        pl.BlockSpec(taps_x.shape, lambda i, n: (0, 0)),
        pl.BlockSpec(taps_t.shape, lambda i, n: (0, 0)),
    ]
    args = [count, x, w, taps_x, taps_t]
    aliases = {}
    if out is not None:
        in_specs.append(pl.BlockSpec(memory_space=pl.ANY))
        args.append(out)
        aliases = {5: 0}
    return pl.pallas_call(
        functools.partial(interior_kernel, start),
        out_shape=jax.ShapeDtypeStruct(x.shape, BF16),
        grid_spec=pltpu.PrefetchScalarGridSpec(
            num_scalar_prefetch=1,
            grid=(steps,),
            in_specs=in_specs,
            out_specs=pl.BlockSpec((1, block, samples), lambda i, n: (i + start, 0, 0)),
            scratch_shapes=[
                pltpu.VMEM((2, block, samples), BF16),
                pltpu.VMEM((inner, samples), BF16),
                pltpu.VMEM((inner, block), BF16),
                pltpu.VMEM((dips * PAIR_K // 2, TILE), BF16),
            ],
        ),
        input_output_aliases=aliases,
        compiler_params=params(),
        cost_estimate=cost(steps * 2_000_000_000, steps * 2**20),
        name="interior",
    )(*args)


def edge_kernel(
    groups, count, xt, xb, halo, w, taps_x, taps_t, _, o, shifted, tp, res, xe, m, sems
):
    dips = taps_x.shape[0]
    g = pl.program_id(0)
    per = xt.shape[0]
    samples = xt.shape[2]
    rows = per * 2 * EDGE
    n_slices = halo.shape[0]
    half = xe.shape[0] // 2
    live = g * per < count[0]

    def copies(group):
        slots = pl.ds(group * per, per)
        return (
            pltpu.make_async_copy(
                res.at[group, :, pl.ds(0, EDGE)], o.at[slots, pl.ds(0, EDGE)], sems.at[group, 0]
            ),
            pltpu.make_async_copy(
                res.at[group, :, pl.ds(EDGE, EDGE)],
                o.at[slots, pl.ds(128 - EDGE, EDGE)],
                sems.at[group, 1],
            ),
        )

    @pl.when(g == 0)
    def _():
        fill_time_bands(taps_t, m)
        for i, band in enumerate(trace_bands(taps_x, 64)):
            xe[i * 32 : i * 32 + 16] = band[:16, :96]
            xe[i * 32 + 16 : i * 32 + 32] = band[48:, :96]

    @pl.when(live)
    def _():
        for i in range(per):
            above = [halo[s, i * 32 : i * 32 + EDGE] for s in range(n_slices)]
            below = [halo[s, i * 32 + EDGE : i * 32 + 32] for s in range(n_slices)]
            above = jnp.concatenate(above, axis=1)
            below = jnp.concatenate(below, axis=1)
            for k in range(2):
                by = HALF_T + 64 * k
                shifted[k, i, 0:16] = turned(above, by)
                shifted[k, i, 16:48] = turned(xt[i], by)
                shifted[k, i, 48:80] = turned(xb[i], by)
                shifted[k, i, 80:96] = turned(below, by)
                for lo, hi in column_tiles(samples):
                    part = jnp.dot(
                        xe[k * half : (k + 1) * half],
                        shifted[k, i, :, lo:hi],
                        preferred_element_type=F32,
                    ).astype(BF16)
                    for c in range(dips // 2):
                        at = (k * dips // 2 + c) * rows + i * 32
                        tp[at : at + 32, lo:hi] = part[c * 32 : c * 32 + 32]
        for tile in range(samples // TILE):
            cols = slice(tile * TILE, (tile + 1) * TILE)
            [noise] = noise_tiles(tp, m, dips, rows, (tile,))
            for i in range(per):
                keep = g * per + i < count[0]
                top = noise[i * 32 : i * 32 + 16]
                bottom = noise[i * 32 + 16 : i * 32 + 32]
                wt = jnp.concatenate([w[i, :EDGE]] * 2, axis=1)
                wb = jnp.concatenate([w[i, 128 - EDGE :]] * 2, axis=1)
                top = xt[i, :EDGE, cols].astype(F32) - wt * top
                bottom = xb[i, EDGE:, cols].astype(F32) - wb * bottom
                res[g, i, :EDGE, cols] = jnp.where(keep, top, 0.0).astype(BF16)
                res[g, i, EDGE:, cols] = jnp.where(keep, bottom, 0.0).astype(BF16)
        for copy in copies(g):
            copy.start()

    @pl.when(g == groups - 1)
    def _():
        for group in range(groups):

            @pl.when(group * per < count[0])
            def _():
                for copy in copies(group):
                    copy.wait()


def edges(count, x, halo, w, taps_x, taps_t, out, per=6):
    slots, block, samples = x.shape
    dips = taps_x.shape[0]
    groups = slots // per
    last = lambda g, n: jnp.minimum(g, jnp.maximum(n[0] - 1, 0) // per)
    return pl.pallas_call(
        functools.partial(edge_kernel, groups),
        out_shape=jax.ShapeDtypeStruct(x.shape, BF16),
        grid_spec=pltpu.PrefetchScalarGridSpec(
            num_scalar_prefetch=1,
            grid=(groups,),
            in_specs=[
                pl.BlockSpec((per, 32, samples), lambda g, n: (last(g, n), 0, 0)),
                pl.BlockSpec((per, 32, samples), lambda g, n: (last(g, n), 3, 0)),
                pl.BlockSpec((halo.shape[0], per * 32, 128), lambda g, n: (0, last(g, n), 0)),
                pl.BlockSpec((per, block, 128), lambda g, n: (last(g, n), 0, 0)),
                pl.BlockSpec(taps_x.shape, lambda g, n: (0, 0)),
                pl.BlockSpec(taps_t.shape, lambda g, n: (0, 0)),
                pl.BlockSpec(memory_space=pl.ANY),
            ],
            out_specs=pl.BlockSpec(memory_space=pl.ANY),
            scratch_shapes=[
                pltpu.VMEM((2, per, 96, samples), BF16),
                pltpu.VMEM((dips * per * 32, samples), BF16),
                pltpu.VMEM((groups, per, 32, samples), BF16),
                pltpu.VMEM((dips * 32, 96), BF16),
                pltpu.VMEM((dips * PAIR_K // 2, TILE), BF16),
                pltpu.SemaphoreType.DMA((groups, 2)),
            ],
        ),
        input_output_aliases={7: 0},
        compiler_params=params(EDGE_VMEM),
        cost_estimate=cost(8_000_000_000, 2**23),
        name="edges",
    )(count, x, x, halo, w, taps_x, taps_t, out)


def payload_kernel(per_line, count, dest, offset, xt, xb, o):
    slots = xt.shape[0]
    slot = lax.broadcasted_iota(jnp.int32, (1, slots), 1)
    place = jnp.where(slot < count[0, 0], dest[...] * per_line + offset[...], -2)
    place = jnp.broadcast_to(place.astype(F32), (EDGE, slots)).astype(BF16)
    for s in range(o.shape[0]):
        cols = slice(s * 128, (s + 1) * 128)
        for i in range(slots):
            o[s, i * 32 : i * 32 + EDGE] = xt[i, :, cols]
            o[s, i * 32 + EDGE : i * 32 + 32] = xb[i, :, cols]
        o[s, slots * 32 :, 0:slots] = place


def payload(block_count, slot_dest, slot_offset, x, steps=4):
    slots, block, samples = x.shape
    slices = samples // 128
    per = slices // steps
    return pl.pallas_call(
        functools.partial(payload_kernel, slots // 2),
        out_shape=jax.ShapeDtypeStruct((slices, slots * 32 + EDGE, 128), BF16),
        grid=(steps,),
        in_specs=[
            pl.BlockSpec(memory_space=pltpu.SMEM),
            pl.BlockSpec((1, slots), lambda i: (0, 0)),
            pl.BlockSpec((1, slots), lambda i: (0, 0)),
            pl.BlockSpec((slots, EDGE, per * 128), lambda i: (0, 0, i)),
            pl.BlockSpec((slots, EDGE, per * 128), lambda i: (0, block // EDGE - 1, i)),
        ],
        out_specs=pl.BlockSpec((per, slots * 32 + EDGE, 128), lambda i: (i, 0, 0)),
        compiler_params=params(),
        cost_estimate=cost(0, 2**22),
        name="payload",
    )(block_count, slot_dest, slot_offset, x, x)


def permute_kernel(slots, x, o, places, table, where, sem):
    sources = places.shape[0]
    stride = slots * 32 + EDGE
    for s in range(sources):
        row = x[s * stride + slots * 32 : (s + 1) * stride]
        places[s : s + 1] = row.astype(F32)[:1].astype(jnp.int32)
    copy = pltpu.make_async_copy(places, table, sem)
    copy.start()
    copy.wait()
    total = sources * (slots // 2)
    where[0] = -1
    where[total + 1] = -1

    def fill(s, _):
        for i in range(slots):
            p = table[s, i]
            where[jnp.where(p < 0, total + 2, p + 1)] = s * stride + i * 32
        return 0

    lax.fori_loop(0, sources, fill, 0)

    def move(s, _):
        for i in range(slots):
            p = jnp.maximum(table[s, i], 0)
            a = where[p]
            b = where[p + 2]
            above = x[pl.ds(pl.multiple_of(jnp.maximum(a, 0) + EDGE, EDGE), EDGE)]
            below = x[pl.ds(pl.multiple_of(jnp.maximum(b, 0), EDGE), EDGE)]
            o[s, i * 32 : i * 32 + EDGE] = jnp.where(a >= 0, above, jnp.zeros_like(above))
            o[s, i * 32 + EDGE : i * 32 + 32] = jnp.where(b >= 0, below, jnp.zeros_like(below))
        return 0

    lax.fori_loop(0, sources, move, 0)


def permute(x, slots):
    sources, rows, width = x.shape
    total = sources * (slots // 2)
    return pl.pallas_call(
        functools.partial(permute_kernel, slots),
        out_shape=jax.ShapeDtypeStruct((sources, slots * 32, width), BF16),
        in_specs=[pl.BlockSpec(memory_space=pltpu.VMEM)],
        out_specs=pl.BlockSpec(memory_space=pltpu.VMEM),
        scratch_shapes=[
            pltpu.VMEM((sources, 128), jnp.int32),
            pltpu.SMEM((sources, 128), jnp.int32),
            pltpu.SMEM((total + 3,), jnp.int32),
            pltpu.SemaphoreType.DMA,
        ],
        compiler_params=pltpu.CompilerParams(vmem_limit_bytes=16 * 2**20),
        cost_estimate=cost(0, 2**23),
        name="permute",
    )(x.reshape(sources * rows, width))


def shards(
    shot_traces, slot_dest, slot_offset, block_count, amp_index, amp_table, dip_trace, dip_time
):
    x = shot_traces[0]
    slots, block, samples = x.shape
    count = block_count.reshape(1)

    ends = payload(block_count, slot_dest, slot_offset, x)
    ends = lax.all_to_all(ends, "rline", split_axis=0, concat_axis=0, tiled=True)

    amps = lax.all_gather(amp_table, "shot", axis=0, tiled=True)
    table_hit = amp_index[0][:, :, None] == jnp.arange(amps.shape[0], dtype=jnp.int32)
    weight = jnp.sum(jnp.where(table_hit, amps, F32(0.0)), axis=2)
    weight = jnp.broadcast_to(weight[:, :, None], (slots, block, 128))
    taps_x, taps_t = spread_taps(dip_trace, dip_time)

    out = interior(count, x, weight, taps_x, taps_t, 0, FIRST)
    ends, out = lax.optimization_barrier((ends, out))
    moved = permute(ends, slots)
    halo = lax.all_to_all(moved, "rline", split_axis=0, concat_axis=0, tiled=True)
    out = interior(count, x, weight, taps_x, taps_t, FIRST, slots - FIRST, out)
    out = edges(count, x, halo, weight, taps_x, taps_t, out)
    return out[None]


def solution(mesh):
    in_specs = (
        P("shot", "rline", None, None),
        P("shot", "rline"),
        P("shot", "rline"),
        P("shot", "rline"),
        P("shot", "rline", None),
        P("shot"),
        P(),
        P(),
    )
    out_specs = P("shot", "rline", None, None)
    return jax.shard_map(shards, mesh=mesh, in_specs=in_specs, out_specs=out_specs, check_vma=False)
```

```python
import functools

import jax
import jax.numpy as jnp
from jax import lax
from jax.experimental import pallas as pl
from jax.experimental.pallas import tpu as pltpu
from jax.sharding import PartitionSpec as P

BF16 = jnp.bfloat16
F32 = jnp.float32
EDGE = 16
TILE = 256
HALF_T = 32
PAIR_K = 640
VMEM_LIMIT = 56 * 2**20
EDGE_VMEM = 50 * 2**20
FIRST = 8


def params(limit=VMEM_LIMIT):
    return pltpu.CompilerParams(dimension_semantics=("arbitrary",), vmem_limit_bytes=limit)


def cost(flops, bytes_accessed):
    return pl.CostEstimate(flops=flops, bytes_accessed=bytes_accessed, transcendentals=0)


def fill_time_bands(taps, m):
    row = lax.broadcasted_iota(jnp.int32, (TILE, TILE), 0)
    col = lax.broadcasted_iota(jnp.int32, (TILE, TILE), 1)
    taps = moved_taps(taps[...], TILE, -1)
    for c in range(taps.shape[0]):
        base = jnp.broadcast_to(taps[c : c + 1], (TILE, TILE))
        band = pltpu.roll(base, 0, 1, stride=1, stride_axis=0)
        at = c * (PAIR_K // 2)
        m[at : at + TILE] = jnp.where(col <= row, band, 0.0).astype(BF16)
        m[at + TILE : at + PAIR_K // 2] = jnp.where(col > row, band, 0.0)[:64].astype(BF16)


def trace_bands(taps, rows):
    dips = taps.shape[0]
    taps = moved_taps(taps[...], 128, 1)
    for c in list(range(0, dips, 2)) + list(range(1, dips, 2)):
        base = jnp.broadcast_to(taps[c : c + 1], (rows, 128))
        yield pltpu.roll(base, 0, 1, stride=1, stride_axis=0).astype(BF16)


def moved_taps(taps, width, sign):
    row = lax.broadcasted_iota(jnp.int32, (taps.shape[1], width), 0)
    col = lax.broadcasted_iota(jnp.int32, (taps.shape[1], width), 1)
    hit = (col == row) if sign > 0 else ((col == 0) & (row == 0)) | (col + row == width)
    return jnp.dot(taps, hit.astype(F32).astype(BF16), preferred_element_type=F32)


def columns(weight):
    return jnp.broadcast_to(weight, (weight.shape[1], weight.shape[1])).T


def turned(x, by):
    return jnp.concatenate([x[:, x.shape[1] - by :], x[:, : x.shape[1] - by]], axis=1)


def time_lhs(tp, dips, rows, tile):
    samples = tp.shape[1]
    lane = lax.broadcasted_iota(jnp.int32, (rows, 128), 1)
    zero = jnp.zeros((rows, 128), BF16)
    first, last = tile == 0, tile == samples // TILE - 1
    at = [(tile * TILE + 128 * k) % samples for k in range(3)]
    parts = []
    for pair in range(dips // 2):
        even = [tp[pl.ds(pair * rows, rows), lo : lo + 128] for lo in at]
        odd = [tp[pl.ds((dips // 2 + pair) * rows, rows), lo : lo + 128] for lo in at]
        if first:
            even[0] = jnp.where(lane < HALF_T, zero, even[0])
            odd[0] = jnp.where(lane < HALF_T + 64, zero, odd[0])
        if last:
            even[2] = jnp.where(lane < HALF_T, even[2], zero)
            odd[2] = jnp.where(lane < HALF_T + 64, odd[2], zero)
        parts += [even[0], even[1], jnp.where(lane < 64, even[2], odd[0]), odd[1], odd[2]]
    return jnp.concatenate(parts, axis=1)


def noise_tiles(tp, m, dips, rows, tiles):
    lhs = jnp.concatenate([time_lhs(tp, dips, rows, tile) for tile in tiles], axis=0)
    noise = jnp.dot(lhs, m[...], preferred_element_type=F32)
    return [noise[k * rows : (k + 1) * rows] for k in range(len(tiles))]


def column_tiles(samples):
    return [(lo, lo + TILE) for lo in range(0, samples, TILE)]


def interior_kernel(start, count, x, w, taps_x, taps_t, *refs):
    o, shifted, tp, xi, m = refs[-5:]
    dips = taps_x.shape[0]
    rows = x.shape[1] - 2 * EDGE
    samples = x.shape[2]
    half = dips // 2 * rows
    slot = pl.program_id(0) + start

    @pl.when(pl.program_id(0) == 0)
    def _():
        fill_time_bands(taps_t, m)
        for i, band in enumerate(trace_bands(taps_x, rows)):
            xi[i * rows : (i + 1) * rows] = band

    @pl.when(slot < count[0])
    def _():
        for k in range(2):
            shifted[k] = turned(x[0], HALF_T + 64 * k)
        for k in range(2):
            for lo, hi in column_tiles(samples):
                tp[k * half : (k + 1) * half, lo:hi] = jnp.dot(
                    xi[k * half : (k + 1) * half],
                    shifted[k, :, lo:hi],
                    preferred_element_type=F32,
                ).astype(BF16)
        weight = jnp.concatenate([columns(w[0])[EDGE : EDGE + rows]] * 2, axis=1)
        for first in range(0, samples // TILE, 2):
            tiles = (first, first + 1)
            for tile, noise in zip(tiles, noise_tiles(tp, m, dips, rows, tiles)):
                cols = slice(tile * TILE, (tile + 1) * TILE)
                center = x[0, EDGE : EDGE + rows, cols].astype(F32)
                o[0, EDGE : EDGE + rows, cols] = (center - weight * noise).astype(BF16)

    @pl.when(slot >= count[0])
    def _():
        o[...] = jnp.zeros_like(o)


def interior(count, x, w, taps_x, taps_t, start, steps, out=None):
    slots, block, samples = x.shape
    dips = taps_x.shape[0]
    inner = dips * (block - 2 * EDGE)
    fetch = lambda i, n: (jnp.minimum(i + start, jnp.maximum(n[0] - 1, 0)), 0, 0)
    in_specs = [
        pl.BlockSpec((1, block, samples), fetch),
        pl.BlockSpec((1, 1, block), fetch),
        pl.BlockSpec(taps_x.shape, lambda i, n: (0, 0)),
        pl.BlockSpec(taps_t.shape, lambda i, n: (0, 0)),
    ]
    args = [count, x, w, taps_x, taps_t]
    aliases = {}
    if out is not None:
        in_specs.append(pl.BlockSpec(memory_space=pl.ANY))
        args.append(out)
        aliases = {5: 0}
    return pl.pallas_call(
        functools.partial(interior_kernel, start),
        out_shape=jax.ShapeDtypeStruct(x.shape, BF16),
        grid_spec=pltpu.PrefetchScalarGridSpec(
            num_scalar_prefetch=1,
            grid=(steps,),
            in_specs=in_specs,
            out_specs=pl.BlockSpec((1, block, samples), lambda i, n: (i + start, 0, 0)),
            scratch_shapes=[
                pltpu.VMEM((2, block, samples), BF16),
                pltpu.VMEM((inner, samples), BF16),
                pltpu.VMEM((inner, block), BF16),
                pltpu.VMEM((dips * PAIR_K // 2, TILE), BF16),
            ],
        ),
        input_output_aliases=aliases,
        compiler_params=params(),
        cost_estimate=cost(steps * 2_000_000_000, steps * 2**20),
        name="interior",
    )(*args)


def edge_kernel(
    groups, count, xt, xb, halo, w, taps_x, taps_t, _, o, shifted, tp, res, xe, m, sems
):
    dips = taps_x.shape[0]
    g = pl.program_id(0)
    per = xt.shape[0]
    samples = xt.shape[2]
    rows = per * 2 * EDGE
    n_slices = halo.shape[0]
    half = xe.shape[0] // 2
    live = g * per < count[0]

    def copies(group):
        slots = pl.ds(group * per, per)
        return (
            pltpu.make_async_copy(
                res.at[group, :, pl.ds(0, EDGE)], o.at[slots, pl.ds(0, EDGE)], sems.at[group, 0]
            ),
            pltpu.make_async_copy(
                res.at[group, :, pl.ds(EDGE, EDGE)],
                o.at[slots, pl.ds(128 - EDGE, EDGE)],
                sems.at[group, 1],
            ),
        )

    @pl.when(g == 0)
    def _():
        fill_time_bands(taps_t, m)
        for i, band in enumerate(trace_bands(taps_x, 64)):
            xe[i * 32 : i * 32 + 16] = band[:16, :96]
            xe[i * 32 + 16 : i * 32 + 32] = band[48:, :96]

    @pl.when(live)
    def _():
        for i in range(per):
            above = [halo[s, i * 32 : i * 32 + EDGE] for s in range(n_slices)]
            below = [halo[s, i * 32 + EDGE : i * 32 + 32] for s in range(n_slices)]
            above = jnp.concatenate(above, axis=1)
            below = jnp.concatenate(below, axis=1)
            for k in range(2):
                by = HALF_T + 64 * k
                shifted[k, i, 0:16] = turned(above, by)
                shifted[k, i, 16:48] = turned(xt[i], by)
                shifted[k, i, 48:80] = turned(xb[i], by)
                shifted[k, i, 80:96] = turned(below, by)
                for lo, hi in column_tiles(samples):
                    part = jnp.dot(
                        xe[k * half : (k + 1) * half],
                        shifted[k, i, :, lo:hi],
                        preferred_element_type=F32,
                    ).astype(BF16)
                    for c in range(dips // 2):
                        at = (k * dips // 2 + c) * rows + i * 32
                        tp[at : at + 32, lo:hi] = part[c * 32 : c * 32 + 32]
        weights = [columns(w[i]) for i in range(per)]
        tops = [jnp.concatenate([weight[:EDGE]] * 2, axis=1) for weight in weights]
        bottoms = [jnp.concatenate([weight[128 - EDGE :]] * 2, axis=1) for weight in weights]
        for tile in range(samples // TILE):
            cols = slice(tile * TILE, (tile + 1) * TILE)
            [noise] = noise_tiles(tp, m, dips, rows, (tile,))
            for i in range(per):
                keep = g * per + i < count[0]
                top = noise[i * 32 : i * 32 + 16]
                bottom = noise[i * 32 + 16 : i * 32 + 32]
                top = xt[i, :EDGE, cols].astype(F32) - tops[i] * top
                bottom = xb[i, EDGE:, cols].astype(F32) - bottoms[i] * bottom
                res[g, i, :EDGE, cols] = jnp.where(keep, top, 0.0).astype(BF16)
                res[g, i, EDGE:, cols] = jnp.where(keep, bottom, 0.0).astype(BF16)
        for copy in copies(g):
            copy.start()

    @pl.when(g == groups - 1)
    def _():
        for group in range(groups):

            @pl.when(group * per < count[0])
            def _():
                for copy in copies(group):
                    copy.wait()


def edges(count, x, halo, w, taps_x, taps_t, out, per=6):
    slots, block, samples = x.shape
    dips = taps_x.shape[0]
    groups = slots // per
    last = lambda g, n: jnp.minimum(g, jnp.maximum(n[0] - 1, 0) // per)
    return pl.pallas_call(
        functools.partial(edge_kernel, groups),
        out_shape=jax.ShapeDtypeStruct(x.shape, BF16),
        grid_spec=pltpu.PrefetchScalarGridSpec(
            num_scalar_prefetch=1,
            grid=(groups,),
            in_specs=[
                pl.BlockSpec((per, 32, samples), lambda g, n: (last(g, n), 0, 0)),
                pl.BlockSpec((per, 32, samples), lambda g, n: (last(g, n), 3, 0)),
                pl.BlockSpec((halo.shape[0], per * 32, 128), lambda g, n: (0, last(g, n), 0)),
                pl.BlockSpec((per, 1, block), lambda g, n: (last(g, n), 0, 0)),
                pl.BlockSpec(taps_x.shape, lambda g, n: (0, 0)),
                pl.BlockSpec(taps_t.shape, lambda g, n: (0, 0)),
                pl.BlockSpec(memory_space=pl.ANY),
            ],
            out_specs=pl.BlockSpec(memory_space=pl.ANY),
            scratch_shapes=[
                pltpu.VMEM((2, per, 96, samples), BF16),
                pltpu.VMEM((dips * per * 32, samples), BF16),
                pltpu.VMEM((groups, per, 32, samples), BF16),
                pltpu.VMEM((dips * 32, 96), BF16),
                pltpu.VMEM((dips * PAIR_K // 2, TILE), BF16),
                pltpu.SemaphoreType.DMA((groups, 2)),
            ],
        ),
        input_output_aliases={7: 0},
        compiler_params=params(EDGE_VMEM),
        cost_estimate=cost(8_000_000_000, 2**23),
        name="edges",
    )(count, x, x, halo, w, taps_x, taps_t, out)


def payload_kernel(per_line, count, dest, offset, xt, xb, o):
    slots = xt.shape[0]
    slot = lax.broadcasted_iota(jnp.int32, (1, slots), 1)
    place = jnp.where(slot < count[0, 0], dest[...] * per_line + offset[...], -2)
    place = jnp.broadcast_to(place.astype(F32), (EDGE, slots)).astype(BF16)
    for s in range(o.shape[0]):
        cols = slice(s * 128, (s + 1) * 128)
        for i in range(slots):
            o[s, i * 32 : i * 32 + EDGE] = xt[i, :, cols]
            o[s, i * 32 + EDGE : i * 32 + 32] = xb[i, :, cols]
        o[s, slots * 32 :, 0:slots] = place


def payload(block_count, slot_dest, slot_offset, x, steps=2):
    slots, block, samples = x.shape
    slices = samples // 128
    per = slices // steps
    return pl.pallas_call(
        functools.partial(payload_kernel, slots // 2),
        out_shape=jax.ShapeDtypeStruct((slices, slots * 32 + EDGE, 128), BF16),
        grid=(steps,),
        in_specs=[
            pl.BlockSpec(memory_space=pltpu.SMEM),
            pl.BlockSpec((1, slots), lambda i: (0, 0)),
            pl.BlockSpec((1, slots), lambda i: (0, 0)),
            pl.BlockSpec((slots, EDGE, per * 128), lambda i: (0, 0, i)),
            pl.BlockSpec((slots, EDGE, per * 128), lambda i: (0, block // EDGE - 1, i)),
        ],
        out_specs=pl.BlockSpec((per, slots * 32 + EDGE, 128), lambda i: (i, 0, 0)),
        compiler_params=params(),
        cost_estimate=cost(0, 2**22),
        name="payload",
    )(block_count, slot_dest, slot_offset, x, x)


def permute_kernel(slots, x, o, places, table, where, sem):
    sources = places.shape[0]
    stride = slots * 32 + EDGE
    for s in range(sources):
        row = x[s * stride + slots * 32 : (s + 1) * stride]
        places[s : s + 1] = row.astype(F32)[:1].astype(jnp.int32)
    copy = pltpu.make_async_copy(places, table, sem)
    copy.start()
    copy.wait()
    total = sources * (slots // 2)
    where[0] = -1
    where[total + 1] = -1

    def fill(s, _):
        for i in range(slots):
            p = table[s, i]
            where[jnp.where(p < 0, total + 2, p + 1)] = s * stride + i * 32
        return 0

    lax.fori_loop(0, sources, fill, 0)

    def move(s, _):
        for i in range(slots):
            p = jnp.maximum(table[s, i], 0)
            a = where[p]
            b = where[p + 2]
            above = x[pl.ds(pl.multiple_of(jnp.maximum(a, 0) + EDGE, EDGE), EDGE)]
            below = x[pl.ds(pl.multiple_of(jnp.maximum(b, 0), EDGE), EDGE)]
            o[s, i * 32 : i * 32 + EDGE] = jnp.where(a >= 0, above, jnp.zeros_like(above))
            o[s, i * 32 + EDGE : i * 32 + 32] = jnp.where(b >= 0, below, jnp.zeros_like(below))
        return 0

    lax.fori_loop(0, sources, move, 0)


def permute(x, slots):
    sources, rows, width = x.shape
    total = sources * (slots // 2)
    return pl.pallas_call(
        functools.partial(permute_kernel, slots),
        out_shape=jax.ShapeDtypeStruct((sources, slots * 32, width), BF16),
        in_specs=[pl.BlockSpec(memory_space=pltpu.VMEM)],
        out_specs=pl.BlockSpec(memory_space=pltpu.VMEM),
        scratch_shapes=[
            pltpu.VMEM((sources, 128), jnp.int32),
            pltpu.SMEM((sources, 128), jnp.int32),
            pltpu.SMEM((total + 3,), jnp.int32),
            pltpu.SemaphoreType.DMA,
        ],
        compiler_params=pltpu.CompilerParams(vmem_limit_bytes=16 * 2**20),
        cost_estimate=cost(0, 2**23),
        name="permute",
    )(x.reshape(sources * rows, width))


def shards(
    shot_traces, slot_dest, slot_offset, block_count, amp_index, amp_table, dip_trace, dip_time
):
    x = shot_traces[0]
    slots, block, samples = x.shape
    count = block_count.reshape(1)

    ends = payload(block_count, slot_dest, slot_offset, x)
    ends = lax.all_to_all(ends, "rline", split_axis=0, concat_axis=0, tiled=True)

    amps = lax.all_gather(amp_table, "shot", axis=0, tiled=True)
    table_hit = amp_index[0][:, :, None] == jnp.arange(amps.shape[0], dtype=jnp.int32)
    weight = jnp.sum(jnp.where(table_hit, amps, F32(0.0)), axis=2)[:, None]

    out = interior(count, x, weight, dip_trace, dip_time, 0, FIRST)
    ends, out = lax.optimization_barrier((ends, out))
    moved = permute(ends, slots)
    halo = lax.all_to_all(moved, "rline", split_axis=0, concat_axis=0, tiled=True)
    out = interior(count, x, weight, dip_trace, dip_time, FIRST, slots - FIRST, out)
    out = edges(count, x, halo, weight, dip_trace, dip_time, out)
    return out[None]


def solution(mesh):
    in_specs = (
        P("shot", "rline", None, None),
        P("shot", "rline"),
        P("shot", "rline"),
        P("shot", "rline"),
        P("shot", "rline", None),
        P("shot"),
        P(),
        P(),
    )
    out_specs = P("shot", "rline", None, None)
    return jax.shard_map(shards, mesh=mesh, in_specs=in_specs, out_specs=out_specs, check_vma=False)
```

```python
import functools

import jax
import jax.numpy as jnp
from jax import lax
from jax.experimental import pallas as pl
from jax.experimental.pallas import tpu as pltpu
from jax.sharding import PartitionSpec as P

BF16 = jnp.bfloat16
F32 = jnp.float32
EDGE = 16
TILE = 256
HALF_T = 32
PAIR_K = 640
VMEM_LIMIT = 56 * 2**20
EDGE_VMEM = 50 * 2**20
FIRST = 7


def params(limit=VMEM_LIMIT):
    return pltpu.CompilerParams(dimension_semantics=("arbitrary",), vmem_limit_bytes=limit)


def cost(flops, bytes_accessed):
    return pl.CostEstimate(flops=flops, bytes_accessed=bytes_accessed, transcendentals=0)


def fill_time_bands(taps, m):
    row = lax.broadcasted_iota(jnp.int32, (TILE, TILE), 0)
    col = lax.broadcasted_iota(jnp.int32, (TILE, TILE), 1)
    taps = moved_taps(taps[...], TILE, -1)
    for c in range(taps.shape[0]):
        base = jnp.broadcast_to(taps[c : c + 1], (TILE, TILE))
        band = pltpu.roll(base, 0, 1, stride=1, stride_axis=0)
        at = c * (PAIR_K // 2)
        m[at : at + TILE] = jnp.where(col <= row, band, 0.0).astype(BF16)
        m[at + TILE : at + PAIR_K // 2] = jnp.where(col > row, band, 0.0)[:64].astype(BF16)


def trace_bands(taps, rows):
    dips = taps.shape[0]
    taps = moved_taps(taps[...], 128, 1)
    for c in list(range(0, dips, 2)) + list(range(1, dips, 2)):
        base = jnp.broadcast_to(taps[c : c + 1], (rows, 128))
        yield pltpu.roll(base, 0, 1, stride=1, stride_axis=0).astype(BF16)


def moved_taps(taps, width, sign):
    row = lax.broadcasted_iota(jnp.int32, (taps.shape[1], width), 0)
    col = lax.broadcasted_iota(jnp.int32, (taps.shape[1], width), 1)
    hit = (col == row) if sign > 0 else ((col == 0) & (row == 0)) | (col + row == width)
    return jnp.dot(taps, hit.astype(F32).astype(BF16), preferred_element_type=F32)


def columns(weight):
    return jnp.broadcast_to(weight, (weight.shape[1], weight.shape[1])).T


def turned(x, by):
    return jnp.concatenate([x[:, x.shape[1] - by :], x[:, : x.shape[1] - by]], axis=1)


def time_lhs(tp, dips, rows, tile):
    samples = tp.shape[1]
    lane = lax.broadcasted_iota(jnp.int32, (rows, 128), 1)
    zero = jnp.zeros((rows, 128), BF16)
    first, last = tile == 0, tile == samples // TILE - 1
    at = [(tile * TILE + 128 * k) % samples for k in range(3)]
    parts = []
    for pair in range(dips // 2):
        even = [tp[pl.ds(pair * rows, rows), lo : lo + 128] for lo in at]
        odd = [tp[pl.ds((dips // 2 + pair) * rows, rows), lo : lo + 128] for lo in at]
        if first:
            even[0] = jnp.where(lane < HALF_T, zero, even[0])
            odd[0] = jnp.where(lane < HALF_T + 64, zero, odd[0])
        if last:
            even[2] = jnp.where(lane < HALF_T, even[2], zero)
            odd[2] = jnp.where(lane < HALF_T + 64, odd[2], zero)
        parts += [even[0], even[1], jnp.where(lane < 64, even[2], odd[0]), odd[1], odd[2]]
    return jnp.concatenate(parts, axis=1)


def noise_tiles(tp, m, dips, rows, tiles):
    lhs = jnp.concatenate([time_lhs(tp, dips, rows, tile) for tile in tiles], axis=0)
    noise = jnp.dot(lhs, m[...], preferred_element_type=F32)
    return [noise[k * rows : (k + 1) * rows] for k in range(len(tiles))]


def column_tiles(samples):
    return [(lo, lo + TILE) for lo in range(0, samples, TILE)]


def interior_kernel(start, count, x, w, taps_x, taps_t, *refs):
    o, shifted, tp, xi, m = refs[-5:]
    dips = taps_x.shape[0]
    rows = x.shape[1] - 2 * EDGE
    samples = x.shape[2]
    half = dips // 2 * rows
    slot = pl.program_id(0) + start

    @pl.when(pl.program_id(0) == 0)
    def _():
        fill_time_bands(taps_t, m)
        for i, band in enumerate(trace_bands(taps_x, rows)):
            xi[i * rows : (i + 1) * rows] = band

    @pl.when(slot < count[0])
    def _():
        for k in range(2):
            shifted[k] = turned(x[0], HALF_T + 64 * k)
        for k in range(2):
            for lo, hi in column_tiles(samples):
                tp[k * half : (k + 1) * half, lo:hi] = jnp.dot(
                    xi[k * half : (k + 1) * half],
                    shifted[k, :, lo:hi],
                    preferred_element_type=F32,
                ).astype(BF16)
        weight = jnp.concatenate([columns(w[0])[EDGE : EDGE + rows]] * 2, axis=1)
        for first in range(0, samples // TILE, 2):
            tiles = (first, first + 1)
            for tile, noise in zip(tiles, noise_tiles(tp, m, dips, rows, tiles)):
                cols = slice(tile * TILE, (tile + 1) * TILE)
                center = x[0, EDGE : EDGE + rows, cols].astype(F32)
                o[0, EDGE : EDGE + rows, cols] = (center - weight * noise).astype(BF16)

    @pl.when(slot >= count[0])
    def _():
        o[...] = jnp.zeros_like(o)


def interior(count, x, w, taps_x, taps_t, start, steps, out=None):
    slots, block, samples = x.shape
    dips = taps_x.shape[0]
    inner = dips * (block - 2 * EDGE)
    fetch = lambda i, n: (jnp.minimum(i + start, jnp.maximum(n[0] - 1, 0)), 0, 0)
    in_specs = [
        pl.BlockSpec((1, block, samples), fetch),
        pl.BlockSpec((1, 1, block), fetch),
        pl.BlockSpec(taps_x.shape, lambda i, n: (0, 0)),
        pl.BlockSpec(taps_t.shape, lambda i, n: (0, 0)),
    ]
    args = [count, x, w, taps_x, taps_t]
    aliases = {}
    if out is not None:
        in_specs.append(pl.BlockSpec(memory_space=pl.ANY))
        args.append(out)
        aliases = {5: 0}
    return pl.pallas_call(
        functools.partial(interior_kernel, start),
        out_shape=jax.ShapeDtypeStruct(x.shape, BF16),
        grid_spec=pltpu.PrefetchScalarGridSpec(
            num_scalar_prefetch=1,
            grid=(steps,),
            in_specs=in_specs,
            out_specs=pl.BlockSpec((1, block, samples), lambda i, n: (i + start, 0, 0)),
            scratch_shapes=[
                pltpu.VMEM((2, block, samples), BF16),
                pltpu.VMEM((inner, samples), BF16),
                pltpu.VMEM((inner, block), BF16),
                pltpu.VMEM((dips * PAIR_K // 2, TILE), BF16),
            ],
        ),
        input_output_aliases=aliases,
        compiler_params=params(),
        cost_estimate=cost(steps * 2_000_000_000, steps * 2**20),
        name="interior",
    )(*args)


def edge_kernel(
    groups, count, x, halo, w, taps_x, taps_t, _, o, shifted, tp, res, xe, m, own, sems, own_sems
):
    dips = taps_x.shape[0]
    g = pl.program_id(0)
    per = x.shape[0] // groups
    block, samples = x.shape[1:]
    rows = per * 2 * EDGE
    n_slices = halo.shape[0]
    half = xe.shape[0] // 2
    live = g * per < count[0]

    def copies(group):
        slots = pl.ds(group * per, per)
        return (
            pltpu.make_async_copy(
                res.at[group, :, pl.ds(0, EDGE)], o.at[slots, pl.ds(0, EDGE)], sems.at[group, 0]
            ),
            pltpu.make_async_copy(
                res.at[group, :, pl.ds(EDGE, EDGE)],
                o.at[slots, pl.ds(128 - EDGE, EDGE)],
                sems.at[group, 1],
            ),
        )

    def loads(group):
        slots = pl.ds(group * per, per)
        return [
            pltpu.make_async_copy(
                x.at[slots, pl.ds(k * (block - 32), 32)], own.at[k, slots], own_sems.at[group, k]
            )
            for k in range(2)
        ]

    @pl.when(g == 0)
    def _():
        for group in range(groups):

            @pl.when(group * per < count[0])
            def _():
                for load in loads(group):
                    load.start()

        fill_time_bands(taps_t, m)
        for i, band in enumerate(trace_bands(taps_x, 64)):
            xe[i * 32 : i * 32 + 16] = band[:16, :96]
            xe[i * 32 + 16 : i * 32 + 32] = band[48:, :96]

    @pl.when(live)
    def _():
        for load in loads(g):
            load.wait()
        xt = own.at[0, pl.ds(g * per, per)]
        xb = own.at[1, pl.ds(g * per, per)]
        for i in range(per):
            above = [halo[s, i * 32 : i * 32 + EDGE] for s in range(n_slices)]
            below = [halo[s, i * 32 + EDGE : i * 32 + 32] for s in range(n_slices)]
            above = jnp.concatenate(above, axis=1)
            below = jnp.concatenate(below, axis=1)
            for k in range(2):
                by = HALF_T + 64 * k
                shifted[k, i, 0:16] = turned(above, by)
                shifted[k, i, 16:48] = turned(xt[i], by)
                shifted[k, i, 48:80] = turned(xb[i], by)
                shifted[k, i, 80:96] = turned(below, by)
                for lo, hi in column_tiles(samples):
                    part = jnp.dot(
                        xe[k * half : (k + 1) * half],
                        shifted[k, i, :, lo:hi],
                        preferred_element_type=F32,
                    ).astype(BF16)
                    for c in range(dips // 2):
                        at = (k * dips // 2 + c) * rows + i * 32
                        tp[at : at + 32, lo:hi] = part[c * 32 : c * 32 + 32]
        weights = [columns(w[i]) for i in range(per)]
        tops = [jnp.concatenate([weight[:EDGE]] * 2, axis=1) for weight in weights]
        bottoms = [jnp.concatenate([weight[128 - EDGE :]] * 2, axis=1) for weight in weights]
        for tile in range(samples // TILE):
            cols = slice(tile * TILE, (tile + 1) * TILE)
            [noise] = noise_tiles(tp, m, dips, rows, (tile,))
            for i in range(per):
                keep = g * per + i < count[0]
                top = noise[i * 32 : i * 32 + 16]
                bottom = noise[i * 32 + 16 : i * 32 + 32]
                top = xt[i, :EDGE, cols].astype(F32) - tops[i] * top
                bottom = xb[i, EDGE:, cols].astype(F32) - bottoms[i] * bottom
                res[g, i, :EDGE, cols] = jnp.where(keep, top, 0.0).astype(BF16)
                res[g, i, EDGE:, cols] = jnp.where(keep, bottom, 0.0).astype(BF16)
        for copy in copies(g):
            copy.start()

    @pl.when(g == groups - 1)
    def _():
        for group in range(groups):

            @pl.when(group * per < count[0])
            def _():
                for copy in copies(group):
                    copy.wait()


def edges(count, x, halo, w, taps_x, taps_t, out, per=6):
    slots, block, samples = x.shape
    dips = taps_x.shape[0]
    groups = slots // per
    last = lambda g, n: jnp.minimum(g, jnp.maximum(n[0] - 1, 0) // per)
    return pl.pallas_call(
        functools.partial(edge_kernel, groups),
        out_shape=jax.ShapeDtypeStruct(x.shape, BF16),
        grid_spec=pltpu.PrefetchScalarGridSpec(
            num_scalar_prefetch=1,
            grid=(groups,),
            in_specs=[
                pl.BlockSpec(memory_space=pl.ANY),
                pl.BlockSpec((halo.shape[0], per * 32, 128), lambda g, n: (0, last(g, n), 0)),
                pl.BlockSpec((per, 1, block), lambda g, n: (last(g, n), 0, 0)),
                pl.BlockSpec(taps_x.shape, lambda g, n: (0, 0)),
                pl.BlockSpec(taps_t.shape, lambda g, n: (0, 0)),
                pl.BlockSpec(memory_space=pl.ANY),
            ],
            out_specs=pl.BlockSpec(memory_space=pl.ANY),
            scratch_shapes=[
                pltpu.VMEM((2, per, 96, samples), BF16),
                pltpu.VMEM((dips * per * 32, samples), BF16),
                pltpu.VMEM((groups, per, 32, samples), BF16),
                pltpu.VMEM((dips * 32, 96), BF16),
                pltpu.VMEM((dips * PAIR_K // 2, TILE), BF16),
                pltpu.VMEM((2, slots, 32, samples), BF16),
                pltpu.SemaphoreType.DMA((groups, 2)),
                pltpu.SemaphoreType.DMA((groups, 2)),
            ],
        ),
        input_output_aliases={6: 0},
        compiler_params=params(EDGE_VMEM),
        cost_estimate=cost(8_000_000_000, 2**23),
        name="edges",
    )(count, x, halo, w, taps_x, taps_t, out)


def payload_kernel(per_line, count, dest, offset, xt, xb, o):
    slots = xt.shape[0]
    slot = lax.broadcasted_iota(jnp.int32, (1, slots), 1)
    place = jnp.where(slot < count[0, 0], dest[...] * per_line + offset[...], -2).astype(F32)
    place = jnp.concatenate([place, jnp.zeros((1, 128 - slots), F32)], axis=1)
    place = jnp.broadcast_to(place, (EDGE, 128)).astype(BF16)
    row = lax.broadcasted_iota(jnp.int32, (EDGE, 128), 0)
    for s in range(o.shape[0]):
        cols = slice(s * 128, (s + 1) * 128)
        for i in range(slots):
            top = xt[i, :, cols]
            o[s, i * 32 : i * 32 + EDGE] = jnp.where(row < EDGE - 1, top, place) if i == 0 else top
            o[s, i * 32 + EDGE : i * 32 + 32] = xb[i, :, cols]


def payload(block_count, slot_dest, slot_offset, x, steps=2):
    slots, block, samples = x.shape
    slices = samples // 128
    per = slices // steps
    return pl.pallas_call(
        functools.partial(payload_kernel, slots // 2),
        out_shape=jax.ShapeDtypeStruct((slices, slots * 32, 128), BF16),
        grid=(steps,),
        in_specs=[
            pl.BlockSpec(memory_space=pltpu.SMEM),
            pl.BlockSpec((1, slots), lambda i: (0, 0)),
            pl.BlockSpec((1, slots), lambda i: (0, 0)),
            pl.BlockSpec((slots, EDGE, per * 128), lambda i: (0, 0, i)),
            pl.BlockSpec((slots, EDGE, per * 128), lambda i: (0, block // EDGE - 1, i)),
        ],
        out_specs=pl.BlockSpec((per, slots * 32, 128), lambda i: (i, 0, 0)),
        compiler_params=params(),
        cost_estimate=cost(0, 2**22),
        name="payload",
    )(block_count, slot_dest, slot_offset, x, x)


def permute_kernel(slots, x, o, places, table, where, sem):
    sources = places.shape[0]
    stride = slots * 32
    for s in range(sources):
        rows = x[s * stride : s * stride + EDGE].astype(F32)
        places[s : s + 1] = rows[EDGE - 1 :].astype(jnp.int32)
    copy = pltpu.make_async_copy(places, table, sem)
    copy.start()
    copy.wait()
    total = sources * (slots // 2)
    where[0] = -1
    where[total + 1] = -1

    def fill(s, _):
        for i in range(slots):
            p = table[s, i]
            where[jnp.where(p < 0, total + 2, p + 1)] = s * stride + i * 32
        return 0

    lax.fori_loop(0, sources, fill, 0)

    def move(s, _):
        for i in range(slots):
            p = jnp.maximum(table[s, i], 0)
            a = where[p]
            b = where[p + 2]
            above = x[pl.ds(pl.multiple_of(jnp.maximum(a, 0) + EDGE, EDGE), EDGE)]
            below = x[pl.ds(pl.multiple_of(jnp.maximum(b, 0), EDGE), EDGE)]
            o[s, i * 32 : i * 32 + EDGE] = jnp.where(a >= 0, above, jnp.zeros_like(above))
            o[s, i * 32 + EDGE : i * 32 + 32] = jnp.where(b >= 0, below, jnp.zeros_like(below))
        return 0

    lax.fori_loop(0, sources, move, 0)


def permute(x, slots):
    sources, rows, width = x.shape
    total = sources * (slots // 2)
    return pl.pallas_call(
        functools.partial(permute_kernel, slots),
        out_shape=jax.ShapeDtypeStruct((sources, slots * 32, width), BF16),
        in_specs=[pl.BlockSpec(memory_space=pltpu.VMEM)],
        out_specs=pl.BlockSpec(memory_space=pltpu.VMEM),
        scratch_shapes=[
            pltpu.VMEM((sources, 128), jnp.int32),
            pltpu.SMEM((sources, 128), jnp.int32),
            pltpu.SMEM((total + 3,), jnp.int32),
            pltpu.SemaphoreType.DMA,
        ],
        compiler_params=pltpu.CompilerParams(vmem_limit_bytes=16 * 2**20),
        cost_estimate=cost(0, 2**23),
        name="permute",
    )(x.reshape(sources * rows, width))


def shards(
    shot_traces, slot_dest, slot_offset, block_count, amp_index, amp_table, dip_trace, dip_time
):
    x = shot_traces[0]
    slots, block, samples = x.shape
    count = block_count.reshape(1)

    ends = payload(block_count, slot_dest, slot_offset, x)
    ends = lax.all_to_all(ends, "rline", split_axis=0, concat_axis=0, tiled=True)

    amps = lax.all_gather(amp_table, "shot", axis=0, tiled=True)
    table_hit = amp_index[0][:, :, None] == jnp.arange(amps.shape[0], dtype=jnp.int32)
    weight = jnp.sum(jnp.where(table_hit, amps, F32(0.0)), axis=2)[:, None]

    out = interior(count, x, weight, dip_trace, dip_time, 0, FIRST)
    ends, out = lax.optimization_barrier((ends, out))
    moved = permute(ends, slots)
    halo = lax.all_to_all(moved, "rline", split_axis=0, concat_axis=0, tiled=True)
    out = interior(count, x, weight, dip_trace, dip_time, FIRST, slots - FIRST, out)
    out = edges(count, x, halo, weight, dip_trace, dip_time, out)
    return out[None]


def solution(mesh):
    in_specs = (
        P("shot", "rline", None, None),
        P("shot", "rline"),
        P("shot", "rline"),
        P("shot", "rline"),
        P("shot", "rline", None),
        P("shot"),
        P(),
        P(),
    )
    out_specs = P("shot", "rline", None, None)
    return jax.shard_map(shards, mesh=mesh, in_specs=in_specs, out_specs=out_specs, check_vma=False)
```

```python
import functools

import jax
import jax.numpy as jnp
from jax import lax
from jax.experimental import pallas as pl
from jax.experimental.pallas import tpu as pltpu
from jax.sharding import PartitionSpec as P

BF16 = jnp.bfloat16
F32 = jnp.float32
EDGE = 16
TILE = 256
HALF_T = 32
PAIR_K = 640
VMEM_LIMIT = 56 * 2**20
EDGE_VMEM = 50 * 2**20
FIRST = 6


def params(limit=VMEM_LIMIT):
    return pltpu.CompilerParams(dimension_semantics=("arbitrary",), vmem_limit_bytes=limit)


def cost(flops, bytes_accessed):
    return pl.CostEstimate(flops=flops, bytes_accessed=bytes_accessed, transcendentals=0)


def fill_time_bands(taps, m):
    row = lax.broadcasted_iota(jnp.int32, (TILE, TILE), 0)
    col = lax.broadcasted_iota(jnp.int32, (TILE, TILE), 1)
    taps = moved_taps(taps[...], TILE, -1)
    for c in range(taps.shape[0]):
        base = jnp.broadcast_to(taps[c : c + 1], (TILE, TILE))
        band = pltpu.roll(base, 0, 1, stride=1, stride_axis=0)
        at = c * (PAIR_K // 2)
        m[at : at + TILE] = jnp.where(col <= row, band, 0.0).astype(BF16)
        m[at + TILE : at + PAIR_K // 2] = jnp.where(col > row, band, 0.0)[:64].astype(BF16)


def trace_bands(taps, rows):
    dips = taps.shape[0]
    taps = moved_taps(taps[...], 128, 1)
    for c in list(range(0, dips, 2)) + list(range(1, dips, 2)):
        base = jnp.broadcast_to(taps[c : c + 1], (rows, 128))
        yield pltpu.roll(base, 0, 1, stride=1, stride_axis=0).astype(BF16)


def moved_taps(taps, width, sign):
    row = lax.broadcasted_iota(jnp.int32, (taps.shape[1], width), 0)
    col = lax.broadcasted_iota(jnp.int32, (taps.shape[1], width), 1)
    hit = (col == row) if sign > 0 else ((col == 0) & (row == 0)) | (col + row == width)
    return jnp.dot(taps, hit.astype(F32).astype(BF16), preferred_element_type=F32)


def columns(weight):
    return jnp.broadcast_to(weight, (weight.shape[1], weight.shape[1])).T


def turned(x, by):
    return jnp.concatenate([x[:, x.shape[1] - by :], x[:, : x.shape[1] - by]], axis=1)


def time_lhs(tp, dips, rows, tile):
    samples = tp.shape[1]
    lane = lax.broadcasted_iota(jnp.int32, (rows, 128), 1)
    zero = jnp.zeros((rows, 128), BF16)
    first, last = tile == 0, tile == samples // TILE - 1
    at = [(tile * TILE + 128 * k) % samples for k in range(3)]
    parts = []
    for pair in range(dips // 2):
        even = [tp[pl.ds(pair * rows, rows), lo : lo + 128] for lo in at]
        odd = [tp[pl.ds((dips // 2 + pair) * rows, rows), lo : lo + 128] for lo in at]
        if first:
            even[0] = jnp.where(lane < HALF_T, zero, even[0])
            odd[0] = jnp.where(lane < HALF_T + 64, zero, odd[0])
        if last:
            even[2] = jnp.where(lane < HALF_T, even[2], zero)
            odd[2] = jnp.where(lane < HALF_T + 64, odd[2], zero)
        parts += [even[0], even[1], jnp.where(lane < 64, even[2], odd[0]), odd[1], odd[2]]
    return jnp.concatenate(parts, axis=1)


def noise_tiles(tp, m, dips, rows, tiles):
    lhs = jnp.concatenate([time_lhs(tp, dips, rows, tile) for tile in tiles], axis=0)
    noise = jnp.dot(lhs, m[...], preferred_element_type=F32)
    return [noise[k * rows : (k + 1) * rows] for k in range(len(tiles))]


def column_tiles(samples):
    return [(lo, lo + TILE) for lo in range(0, samples, TILE)]


def interior_kernel(start, count, x, w, taps_x, taps_t, *refs):
    o, shifted, tp, xi, m = refs[-5:]
    dips = taps_x.shape[0]
    rows = x.shape[1] - 2 * EDGE
    samples = x.shape[2]
    half = dips // 2 * rows
    slot = pl.program_id(0) + start

    @pl.when(pl.program_id(0) == 0)
    def _():
        fill_time_bands(taps_t, m)
        for i, band in enumerate(trace_bands(taps_x, rows)):
            xi[i * rows : (i + 1) * rows] = band

    @pl.when(slot < count[0])
    def _():
        for k in range(2):
            shifted[k] = turned(x[0], HALF_T + 64 * k)
        for k in range(2):
            for lo, hi in column_tiles(samples):
                tp[k * half : (k + 1) * half, lo:hi] = jnp.dot(
                    xi[k * half : (k + 1) * half],
                    shifted[k, :, lo:hi],
                    preferred_element_type=F32,
                ).astype(BF16)
        weight = jnp.concatenate([columns(w[0])[EDGE : EDGE + rows]] * 2, axis=1)
        for first in range(0, samples // TILE, 2):
            tiles = (first, first + 1)
            for tile, noise in zip(tiles, noise_tiles(tp, m, dips, rows, tiles)):
                cols = slice(tile * TILE, (tile + 1) * TILE)
                center = x[0, EDGE : EDGE + rows, cols].astype(F32)
                o[0, EDGE : EDGE + rows, cols] = (center - weight * noise).astype(BF16)

    @pl.when(slot >= count[0])
    def _():
        o[...] = jnp.zeros_like(o)


def interior(count, x, w, taps_x, taps_t, start, steps, out=None):
    slots, block, samples = x.shape
    dips = taps_x.shape[0]
    inner = dips * (block - 2 * EDGE)
    fetch = lambda i, n: (jnp.minimum(i + start, jnp.maximum(n[0] - 1, 0)), 0, 0)
    in_specs = [
        pl.BlockSpec((1, block, samples), fetch),
        pl.BlockSpec((1, 1, block), fetch),
        pl.BlockSpec(taps_x.shape, lambda i, n: (0, 0)),
        pl.BlockSpec(taps_t.shape, lambda i, n: (0, 0)),
    ]
    args = [count, x, w, taps_x, taps_t]
    aliases = {}
    if out is not None:
        in_specs.append(pl.BlockSpec(memory_space=pl.ANY))
        args.append(out)
        aliases = {5: 0}
    return pl.pallas_call(
        functools.partial(interior_kernel, start),
        out_shape=jax.ShapeDtypeStruct(x.shape, BF16),
        grid_spec=pltpu.PrefetchScalarGridSpec(
            num_scalar_prefetch=1,
            grid=(steps,),
            in_specs=in_specs,
            out_specs=pl.BlockSpec((1, block, samples), lambda i, n: (i + start, 0, 0)),
            scratch_shapes=[
                pltpu.VMEM((2, block, samples), BF16),
                pltpu.VMEM((inner, samples), BF16),
                pltpu.VMEM((inner, block), BF16),
                pltpu.VMEM((dips * PAIR_K // 2, TILE), BF16),
            ],
        ),
        input_output_aliases=aliases,
        compiler_params=params(),
        cost_estimate=cost(steps * 2_000_000_000, steps * 2**20),
        name="interior",
    )(*args)


def edge_kernel(
    groups, count, x, halo, w, taps_x, taps_t, _, o, shifted, tp, res, xe, m, own, sems, own_sems
):
    dips = taps_x.shape[0]
    g = pl.program_id(0)
    per = x.shape[0] // groups
    block, samples = x.shape[1:]
    rows = per * 2 * EDGE
    n_slices = halo.shape[0]
    half = xe.shape[0] // 2
    live = g * per < count[0]

    def copies(group):
        slots = pl.ds(group * per, per)
        return (
            pltpu.make_async_copy(
                res.at[group, :, pl.ds(0, EDGE)], o.at[slots, pl.ds(0, EDGE)], sems.at[group, 0]
            ),
            pltpu.make_async_copy(
                res.at[group, :, pl.ds(EDGE, EDGE)],
                o.at[slots, pl.ds(128 - EDGE, EDGE)],
                sems.at[group, 1],
            ),
        )

    def loads(group):
        slots = pl.ds(group * per, per)
        return [
            pltpu.make_async_copy(
                x.at[slots, pl.ds(k * (block - 32), 32)], own.at[k, slots], own_sems.at[group, k]
            )
            for k in range(2)
        ]

    @pl.when(g == 0)
    def _():
        for group in range(groups):

            @pl.when(group * per < count[0])
            def _():
                for load in loads(group):
                    load.start()

        fill_time_bands(taps_t, m)
        for i, band in enumerate(trace_bands(taps_x, 64)):
            xe[i * 32 : i * 32 + 16] = band[:16, :96]
            xe[i * 32 + 16 : i * 32 + 32] = band[48:, :96]

    @pl.when(live)
    def _():
        for load in loads(g):
            load.wait()
        xt = own.at[0, pl.ds(g * per, per)]
        xb = own.at[1, pl.ds(g * per, per)]
        for i in range(per):
            at = pl.multiple_of((g * per + i) * 32, 32)
            above = [halo[s, pl.ds(at, EDGE)] for s in range(n_slices)]
            below = [halo[s, pl.ds(at + EDGE, EDGE)] for s in range(n_slices)]
            above = jnp.concatenate(above, axis=1)
            below = jnp.concatenate(below, axis=1)
            for k in range(2):
                by = HALF_T + 64 * k
                shifted[k, i, 0:16] = turned(above, by)
                shifted[k, i, 16:48] = turned(xt[i], by)
                shifted[k, i, 48:80] = turned(xb[i], by)
                shifted[k, i, 80:96] = turned(below, by)
                for lo, hi in column_tiles(samples):
                    part = jnp.dot(
                        xe[k * half : (k + 1) * half],
                        shifted[k, i, :, lo:hi],
                        preferred_element_type=F32,
                    ).astype(BF16)
                    for c in range(dips // 2):
                        at = (k * dips // 2 + c) * rows + i * 32
                        tp[at : at + 32, lo:hi] = part[c * 32 : c * 32 + 32]
        weights = [columns(w[i]) for i in range(per)]
        tops = [jnp.concatenate([weight[:EDGE]] * 2, axis=1) for weight in weights]
        bottoms = [jnp.concatenate([weight[128 - EDGE :]] * 2, axis=1) for weight in weights]
        for tile in range(samples // TILE):
            cols = slice(tile * TILE, (tile + 1) * TILE)
            [noise] = noise_tiles(tp, m, dips, rows, (tile,))
            for i in range(per):
                keep = g * per + i < count[0]
                top = noise[i * 32 : i * 32 + 16]
                bottom = noise[i * 32 + 16 : i * 32 + 32]
                top = xt[i, :EDGE, cols].astype(F32) - tops[i] * top
                bottom = xb[i, EDGE:, cols].astype(F32) - bottoms[i] * bottom
                res[g, i, :EDGE, cols] = jnp.where(keep, top, 0.0).astype(BF16)
                res[g, i, EDGE:, cols] = jnp.where(keep, bottom, 0.0).astype(BF16)
        for copy in copies(g):
            copy.start()

    @pl.when(g == groups - 1)
    def _():
        for group in range(groups):

            @pl.when(group * per < count[0])
            def _():
                for copy in copies(group):
                    copy.wait()


def edges(count, x, halo, w, taps_x, taps_t, out, per=6):
    slots, block, samples = x.shape
    dips = taps_x.shape[0]
    groups = slots // per
    last = lambda g, n: jnp.minimum(g, jnp.maximum(n[0] - 1, 0) // per)
    return pl.pallas_call(
        functools.partial(edge_kernel, groups),
        out_shape=jax.ShapeDtypeStruct(x.shape, BF16),
        grid_spec=pltpu.PrefetchScalarGridSpec(
            num_scalar_prefetch=1,
            grid=(groups,),
            in_specs=[
                pl.BlockSpec(memory_space=pl.ANY),
                pl.BlockSpec(memory_space=pltpu.VMEM),
                pl.BlockSpec((per, 1, block), lambda g, n: (last(g, n), 0, 0)),
                pl.BlockSpec(taps_x.shape, lambda g, n: (0, 0)),
                pl.BlockSpec(taps_t.shape, lambda g, n: (0, 0)),
                pl.BlockSpec(memory_space=pl.ANY),
            ],
            out_specs=pl.BlockSpec(memory_space=pl.ANY),
            scratch_shapes=[
                pltpu.VMEM((2, per, 96, samples), BF16),
                pltpu.VMEM((dips * per * 32, samples), BF16),
                pltpu.VMEM((groups, per, 32, samples), BF16),
                pltpu.VMEM((dips * 32, 96), BF16),
                pltpu.VMEM((dips * PAIR_K // 2, TILE), BF16),
                pltpu.VMEM((2, slots, 32, samples), BF16),
                pltpu.SemaphoreType.DMA((groups, 2)),
                pltpu.SemaphoreType.DMA((groups, 2)),
            ],
        ),
        input_output_aliases={6: 0},
        compiler_params=params(EDGE_VMEM),
        cost_estimate=cost(8_000_000_000, 2**23),
        name="edges",
    )(count, x, halo, w, taps_x, taps_t, out)


def payload_kernel(per_line, count, dest, offset, xt, xb, o):
    slots = xt.shape[0]
    slot = lax.broadcasted_iota(jnp.int32, (1, slots), 1)
    place = jnp.where(slot < count[0, 0], dest[...] * per_line + offset[...], -2).astype(F32)
    place = jnp.concatenate([place, jnp.zeros((1, 128 - slots), F32)], axis=1)
    place = jnp.broadcast_to(place, (EDGE, 128)).astype(BF16)
    row = lax.broadcasted_iota(jnp.int32, (EDGE, 128), 0)
    for s in range(o.shape[0]):
        cols = slice(s * 128, (s + 1) * 128)
        for i in range(slots):
            top = xt[i, :, cols]
            o[s, i * 32 : i * 32 + EDGE] = jnp.where(row < EDGE - 1, top, place) if i == 0 else top
            o[s, i * 32 + EDGE : i * 32 + 32] = xb[i, :, cols]


def payload(block_count, slot_dest, slot_offset, x, steps=2):
    slots, block, samples = x.shape
    slices = samples // 128
    per = slices // steps
    return pl.pallas_call(
        functools.partial(payload_kernel, slots // 2),
        out_shape=jax.ShapeDtypeStruct((slices, slots * 32, 128), BF16),
        grid=(steps,),
        in_specs=[
            pl.BlockSpec(memory_space=pltpu.SMEM),
            pl.BlockSpec((1, slots), lambda i: (0, 0)),
            pl.BlockSpec((1, slots), lambda i: (0, 0)),
            pl.BlockSpec((slots, EDGE, per * 128), lambda i: (0, 0, i)),
            pl.BlockSpec((slots, EDGE, per * 128), lambda i: (0, block // EDGE - 1, i)),
        ],
        out_specs=pl.BlockSpec((per, slots * 32, 128), lambda i: (i, 0, 0)),
        compiler_params=params(),
        cost_estimate=cost(0, 2**22),
        name="payload",
    )(block_count, slot_dest, slot_offset, x, x)


def permute_kernel(slots, x, o, places, table, where, sem):
    sources = places.shape[0]
    stride = slots * 32
    for s in range(sources):
        rows = x[s * stride : s * stride + EDGE].astype(F32)
        places[s : s + 1] = rows[EDGE - 1 :].astype(jnp.int32)
    copy = pltpu.make_async_copy(places, table, sem)
    copy.start()
    copy.wait()
    total = sources * (slots // 2)
    where[0] = -1
    where[total + 1] = -1

    def fill(s, _):
        for i in range(slots):
            p = table[s, i]
            where[jnp.where(p < 0, total + 2, p + 1)] = s * stride + i * 32
        return 0

    lax.fori_loop(0, sources, fill, 0)

    def move(s, _):
        for i in range(slots):
            p = jnp.maximum(table[s, i], 0)
            a = where[p]
            b = where[p + 2]
            above = x[pl.ds(pl.multiple_of(jnp.maximum(a, 0) + EDGE, EDGE), EDGE)]
            below = x[pl.ds(pl.multiple_of(jnp.maximum(b, 0), EDGE), EDGE)]
            o[s, i * 32 : i * 32 + EDGE] = jnp.where(a >= 0, above, jnp.zeros_like(above))
            o[s, i * 32 + EDGE : i * 32 + 32] = jnp.where(b >= 0, below, jnp.zeros_like(below))
        return 0

    lax.fori_loop(0, sources, move, 0)


def permute(x, slots):
    sources, rows, width = x.shape
    total = sources * (slots // 2)
    return pl.pallas_call(
        functools.partial(permute_kernel, slots),
        out_shape=jax.ShapeDtypeStruct((sources, slots * 32, width), BF16),
        in_specs=[pl.BlockSpec(memory_space=pltpu.VMEM)],
        out_specs=pl.BlockSpec(memory_space=pltpu.VMEM),
        scratch_shapes=[
            pltpu.VMEM((sources, 128), jnp.int32),
            pltpu.SMEM((sources, 128), jnp.int32),
            pltpu.SMEM((total + 3,), jnp.int32),
            pltpu.SemaphoreType.DMA,
        ],
        compiler_params=pltpu.CompilerParams(vmem_limit_bytes=16 * 2**20),
        cost_estimate=cost(0, 2**23),
        name="permute",
    )(x.reshape(sources * rows, width))


def shards(
    shot_traces, slot_dest, slot_offset, block_count, amp_index, amp_table, dip_trace, dip_time
):
    x = shot_traces[0]
    slots, block, samples = x.shape
    count = block_count.reshape(1)

    ends = payload(block_count, slot_dest, slot_offset, x)
    ends = lax.all_to_all(ends, "rline", split_axis=0, concat_axis=0, tiled=True)

    amps = lax.all_gather(amp_table, "shot", axis=0, tiled=True)
    table_hit = amp_index[0][:, :, None] == jnp.arange(amps.shape[0], dtype=jnp.int32)
    weight = jnp.sum(jnp.where(table_hit, amps, F32(0.0)), axis=2)[:, None]

    out = interior(count, x, weight, dip_trace, dip_time, 0, FIRST)
    ends, out = lax.optimization_barrier((ends, out))
    moved = permute(ends, slots)
    halo = lax.all_to_all(moved, "rline", split_axis=0, concat_axis=0, tiled=True)
    out = interior(count, x, weight, dip_trace, dip_time, FIRST, slots - FIRST, out)
    out = edges(count, x, halo, weight, dip_trace, dip_time, out)
    return out[None]


def solution(mesh):
    in_specs = (
        P("shot", "rline", None, None),
        P("shot", "rline"),
        P("shot", "rline"),
        P("shot", "rline"),
        P("shot", "rline", None),
        P("shot"),
        P(),
        P(),
    )
    out_specs = P("shot", "rline", None, None)
    return jax.shard_map(shards, mesh=mesh, in_specs=in_specs, out_specs=out_specs, check_vma=False)
```

```python
import functools

import jax
import jax.numpy as jnp
from jax import lax
from jax.experimental import pallas as pl
from jax.experimental.pallas import tpu as pltpu
from jax.sharding import PartitionSpec as P

BF16 = jnp.bfloat16
F32 = jnp.float32
EDGE = 16
TILE = 256
HALF_T = 32
PAIR_K = 640
VMEM_LIMIT = 56 * 2**20
EDGE_VMEM = 50 * 2**20
FIRST = 6


def params(limit=VMEM_LIMIT):
    return pltpu.CompilerParams(dimension_semantics=("arbitrary",), vmem_limit_bytes=limit)


def cost(flops, bytes_accessed):
    return pl.CostEstimate(flops=flops, bytes_accessed=bytes_accessed, transcendentals=0)


def fill_time_bands(taps, m):
    row = lax.broadcasted_iota(jnp.int32, (TILE, TILE), 0)
    col = lax.broadcasted_iota(jnp.int32, (TILE, TILE), 1)
    taps = moved_taps(taps[...], TILE, -1)
    for c in range(taps.shape[0]):
        base = jnp.broadcast_to(taps[c : c + 1], (TILE, TILE))
        band = pltpu.roll(base, 0, 1, stride=1, stride_axis=0)
        at = c * (PAIR_K // 2)
        m[at : at + TILE] = jnp.where(col <= row, band, 0.0).astype(BF16)
        m[at + TILE : at + PAIR_K // 2] = jnp.where(col > row, band, 0.0)[:64].astype(BF16)


def trace_bands(taps, rows):
    dips = taps.shape[0]
    taps = moved_taps(taps[...], 128, 1)
    for c in list(range(0, dips, 2)) + list(range(1, dips, 2)):
        base = jnp.broadcast_to(taps[c : c + 1], (rows, 128))
        yield pltpu.roll(base, 0, 1, stride=1, stride_axis=0).astype(BF16)


def moved_taps(taps, width, sign):
    row = lax.broadcasted_iota(jnp.int32, (taps.shape[1], width), 0)
    col = lax.broadcasted_iota(jnp.int32, (taps.shape[1], width), 1)
    hit = (col == row) if sign > 0 else ((col == 0) & (row == 0)) | (col + row == width)
    return jnp.dot(taps, hit.astype(F32).astype(BF16), preferred_element_type=F32)


def columns(weight):
    return jnp.broadcast_to(weight, (weight.shape[1], weight.shape[1])).T


def turned(x, by):
    return jnp.concatenate([x[:, x.shape[1] - by :], x[:, : x.shape[1] - by]], axis=1)


def time_lhs(tp, dips, rows, tile):
    samples = tp.shape[1]
    lane = lax.broadcasted_iota(jnp.int32, (rows, 128), 1)
    zero = jnp.zeros((rows, 128), BF16)
    first, last = tile == 0, tile == samples // TILE - 1
    at = [(tile * TILE + 128 * k) % samples for k in range(3)]
    parts = []
    for pair in range(dips // 2):
        even = [tp[pl.ds(pair * rows, rows), lo : lo + 128] for lo in at]
        odd = [tp[pl.ds((dips // 2 + pair) * rows, rows), lo : lo + 128] for lo in at]
        if first:
            even[0] = jnp.where(lane < HALF_T, zero, even[0])
            odd[0] = jnp.where(lane < HALF_T + 64, zero, odd[0])
        if last:
            even[2] = jnp.where(lane < HALF_T, even[2], zero)
            odd[2] = jnp.where(lane < HALF_T + 64, odd[2], zero)
        parts += [even[0], even[1], jnp.where(lane < 64, even[2], odd[0]), odd[1], odd[2]]
    return jnp.concatenate(parts, axis=1)


def noise_tiles(tp, m, dips, rows, tiles):
    lhs = jnp.concatenate([time_lhs(tp, dips, rows, tile) for tile in tiles], axis=0)
    noise = jnp.dot(lhs, m[...], preferred_element_type=F32)
    return [noise[k * rows : (k + 1) * rows] for k in range(len(tiles))]


def column_tiles(samples):
    return [(lo, lo + 2 * TILE) for lo in range(0, samples, 2 * TILE)]


def interior_kernel(start, count, x, w, taps_x, taps_t, *refs):
    o, shifted, tp, xi, m = refs[-5:]
    dips = taps_x.shape[0]
    rows = x.shape[1] - 2 * EDGE
    samples = x.shape[2]
    half = dips // 2 * rows
    slot = pl.program_id(0) + start

    @pl.when(pl.program_id(0) == 0)
    def _():
        fill_time_bands(taps_t, m)
        for i, band in enumerate(trace_bands(taps_x, rows)):
            xi[i * rows : (i + 1) * rows] = band

    @pl.when(slot < count[0])
    def _():
        for k in range(2):
            shifted[k] = turned(x[0], HALF_T + 64 * k)
        for k in range(2):
            for lo, hi in column_tiles(samples):
                tp[k * half : (k + 1) * half, lo:hi] = jnp.dot(
                    xi[k * half : (k + 1) * half],
                    shifted[k, :, lo:hi],
                    preferred_element_type=F32,
                ).astype(BF16)
        weight = jnp.concatenate([columns(w[0])[EDGE : EDGE + rows]] * 2, axis=1)
        for first in range(0, samples // TILE, 2):
            tiles = (first, first + 1)
            for tile, noise in zip(tiles, noise_tiles(tp, m, dips, rows, tiles)):
                cols = slice(tile * TILE, (tile + 1) * TILE)
                center = x[0, EDGE : EDGE + rows, cols].astype(F32)
                o[0, EDGE : EDGE + rows, cols] = (center - weight * noise).astype(BF16)

    @pl.when(slot >= count[0])
    def _():
        o[...] = jnp.zeros_like(o)


def interior(count, x, w, taps_x, taps_t, start, steps, out=None):
    slots, block, samples = x.shape
    dips = taps_x.shape[0]
    inner = dips * (block - 2 * EDGE)
    fetch = lambda i, n: (jnp.minimum(i + start, jnp.maximum(n[0] - 1, 0)), 0, 0)
    in_specs = [
        pl.BlockSpec((1, block, samples), fetch),
        pl.BlockSpec((1, 1, block), fetch),
        pl.BlockSpec(taps_x.shape, lambda i, n: (0, 0)),
        pl.BlockSpec(taps_t.shape, lambda i, n: (0, 0)),
    ]
    args = [count, x, w, taps_x, taps_t]
    aliases = {}
    if out is not None:
        in_specs.append(pl.BlockSpec(memory_space=pl.ANY))
        args.append(out)
        aliases = {5: 0}
    return pl.pallas_call(
        functools.partial(interior_kernel, start),
        out_shape=jax.ShapeDtypeStruct(x.shape, BF16),
        grid_spec=pltpu.PrefetchScalarGridSpec(
            num_scalar_prefetch=1,
            grid=(steps,),
            in_specs=in_specs,
            out_specs=pl.BlockSpec((1, block, samples), lambda i, n: (i + start, 0, 0)),
            scratch_shapes=[
                pltpu.VMEM((2, block, samples), BF16),
                pltpu.VMEM((inner, samples), BF16),
                pltpu.VMEM((inner, block), BF16),
                pltpu.VMEM((dips * PAIR_K // 2, TILE), BF16),
            ],
        ),
        input_output_aliases=aliases,
        compiler_params=params(),
        cost_estimate=cost(steps * 2_000_000_000, steps * 2**20),
        name="interior",
    )(*args)


def edge_kernel(
    groups, count, x, halo, w, taps_x, taps_t, _, o, shifted, tp, res, xe, m, own, sems, own_sems
):
    dips = taps_x.shape[0]
    g = pl.program_id(0)
    per = x.shape[0] // groups
    block, samples = x.shape[1:]
    rows = per * 2 * EDGE
    n_slices = halo.shape[0]
    half = xe.shape[0] // 2
    live = g * per < count[0]

    def copies(group):
        slots = pl.ds(group * per, per)
        return (
            pltpu.make_async_copy(
                res.at[group, :, pl.ds(0, EDGE)], o.at[slots, pl.ds(0, EDGE)], sems.at[group, 0]
            ),
            pltpu.make_async_copy(
                res.at[group, :, pl.ds(EDGE, EDGE)],
                o.at[slots, pl.ds(128 - EDGE, EDGE)],
                sems.at[group, 1],
            ),
        )

    def loads(group):
        slots = pl.ds(group * per, per)
        return [
            pltpu.make_async_copy(
                x.at[slots, pl.ds(k * (block - 32), 32)], own.at[k, slots], own_sems.at[group, k]
            )
            for k in range(2)
        ]

    @pl.when(g == 0)
    def _():
        for group in range(groups):

            @pl.when(group * per < count[0])
            def _():
                for load in loads(group):
                    load.start()

        fill_time_bands(taps_t, m)
        for i, band in enumerate(trace_bands(taps_x, 64)):
            xe[i * 32 : i * 32 + 16] = band[:16, :96]
            xe[i * 32 + 16 : i * 32 + 32] = band[48:, :96]

    @pl.when(live)
    def _():
        for load in loads(g):
            load.wait()
        xt = own.at[0, pl.ds(g * per, per)]
        xb = own.at[1, pl.ds(g * per, per)]
        for i in range(per):
            at = pl.multiple_of((g * per + i) * 32, 32)
            above = [halo[s, pl.ds(at, EDGE)] for s in range(n_slices)]
            below = [halo[s, pl.ds(at + EDGE, EDGE)] for s in range(n_slices)]
            above = jnp.concatenate(above, axis=1)
            below = jnp.concatenate(below, axis=1)
            for k in range(2):
                by = HALF_T + 64 * k
                shifted[k, i, 0:16] = turned(above, by)
                shifted[k, i, 16:48] = turned(xt[i], by)
                shifted[k, i, 48:80] = turned(xb[i], by)
                shifted[k, i, 80:96] = turned(below, by)
                for lo, hi in column_tiles(samples):
                    part = jnp.dot(
                        xe[k * half : (k + 1) * half],
                        shifted[k, i, :, lo:hi],
                        preferred_element_type=F32,
                    ).astype(BF16)
                    for c in range(dips // 2):
                        at = (k * dips // 2 + c) * rows + i * 32
                        tp[at : at + 32, lo:hi] = part[c * 32 : c * 32 + 32]
        weights = [columns(w[i]) for i in range(per)]
        tops = [jnp.concatenate([weight[:EDGE]] * 2, axis=1) for weight in weights]
        bottoms = [jnp.concatenate([weight[128 - EDGE :]] * 2, axis=1) for weight in weights]
        for tile in range(samples // TILE):
            cols = slice(tile * TILE, (tile + 1) * TILE)
            [noise] = noise_tiles(tp, m, dips, rows, (tile,))
            for i in range(per):
                keep = g * per + i < count[0]
                top = noise[i * 32 : i * 32 + 16]
                bottom = noise[i * 32 + 16 : i * 32 + 32]
                top = xt[i, :EDGE, cols].astype(F32) - tops[i] * top
                bottom = xb[i, EDGE:, cols].astype(F32) - bottoms[i] * bottom
                res[g, i, :EDGE, cols] = jnp.where(keep, top, 0.0).astype(BF16)
                res[g, i, EDGE:, cols] = jnp.where(keep, bottom, 0.0).astype(BF16)
        for copy in copies(g):
            copy.start()

    @pl.when(g == groups - 1)
    def _():
        for group in range(groups):

            @pl.when(group * per < count[0])
            def _():
                for copy in copies(group):
                    copy.wait()


def edges(count, x, halo, w, taps_x, taps_t, out, per=6):
    slots, block, samples = x.shape
    dips = taps_x.shape[0]
    groups = slots // per
    last = lambda g, n: jnp.minimum(g, jnp.maximum(n[0] - 1, 0) // per)
    return pl.pallas_call(
        functools.partial(edge_kernel, groups),
        out_shape=jax.ShapeDtypeStruct(x.shape, BF16),
        grid_spec=pltpu.PrefetchScalarGridSpec(
            num_scalar_prefetch=1,
            grid=(groups,),
            in_specs=[
                pl.BlockSpec(memory_space=pl.ANY),
                pl.BlockSpec(memory_space=pltpu.VMEM),
                pl.BlockSpec((per, 1, block), lambda g, n: (last(g, n), 0, 0)),
                pl.BlockSpec(taps_x.shape, lambda g, n: (0, 0)),
                pl.BlockSpec(taps_t.shape, lambda g, n: (0, 0)),
                pl.BlockSpec(memory_space=pl.ANY),
            ],
            out_specs=pl.BlockSpec(memory_space=pl.ANY),
            scratch_shapes=[
                pltpu.VMEM((2, per, 96, samples), BF16),
                pltpu.VMEM((dips * per * 32, samples), BF16),
                pltpu.VMEM((groups, per, 32, samples), BF16),
                pltpu.VMEM((dips * 32, 96), BF16),
                pltpu.VMEM((dips * PAIR_K // 2, TILE), BF16),
                pltpu.VMEM((2, slots, 32, samples), BF16),
                pltpu.SemaphoreType.DMA((groups, 2)),
                pltpu.SemaphoreType.DMA((groups, 2)),
            ],
        ),
        input_output_aliases={6: 0},
        compiler_params=params(EDGE_VMEM),
        cost_estimate=cost(8_000_000_000, 2**23),
        name="edges",
    )(count, x, halo, w, taps_x, taps_t, out)


def payload_kernel(per_line, count, dest, offset, xt, xb, o):
    slots = xt.shape[0]
    slot = lax.broadcasted_iota(jnp.int32, (1, slots), 1)
    place = jnp.where(slot < count[0, 0], dest[...] * per_line + offset[...], -2).astype(F32)
    place = jnp.concatenate([place, jnp.zeros((1, 128 - slots), F32)], axis=1)
    place = jnp.broadcast_to(place, (EDGE, 128)).astype(BF16)
    row = lax.broadcasted_iota(jnp.int32, (EDGE, 128), 0)
    for s in range(o.shape[0]):
        cols = slice(s * 128, (s + 1) * 128)
        for i in range(slots):
            top = xt[i, :, cols]
            o[s, i * 32 : i * 32 + EDGE] = jnp.where(row < EDGE - 1, top, place) if i == 0 else top
            o[s, i * 32 + EDGE : i * 32 + 32] = xb[i, :, cols]


def payload(block_count, slot_dest, slot_offset, x, steps=2):
    slots, block, samples = x.shape
    slices = samples // 128
    per = slices // steps
    return pl.pallas_call(
        functools.partial(payload_kernel, slots // 2),
        out_shape=jax.ShapeDtypeStruct((slices, slots * 32, 128), BF16),
        grid=(steps,),
        in_specs=[
            pl.BlockSpec(memory_space=pltpu.SMEM),
            pl.BlockSpec((1, slots), lambda i: (0, 0)),
            pl.BlockSpec((1, slots), lambda i: (0, 0)),
            pl.BlockSpec((slots, EDGE, per * 128), lambda i: (0, 0, i)),
            pl.BlockSpec((slots, EDGE, per * 128), lambda i: (0, block // EDGE - 1, i)),
        ],
        out_specs=pl.BlockSpec((per, slots * 32, 128), lambda i: (i, 0, 0)),
        compiler_params=params(),
        cost_estimate=cost(0, 2**22),
        name="payload",
    )(block_count, slot_dest, slot_offset, x, x)


def permute_kernel(slots, x, o, places, table, where, sem):
    sources = places.shape[0]
    stride = slots * 32
    for s in range(sources):
        rows = x[s * stride : s * stride + EDGE].astype(F32)
        places[s : s + 1] = rows[EDGE - 1 :].astype(jnp.int32)
    copy = pltpu.make_async_copy(places, table, sem)
    copy.start()
    copy.wait()
    total = sources * (slots // 2)
    where[0] = -1
    where[total + 1] = -1

    def fill(s, _):
        for i in range(slots):
            p = table[s, i]
            where[jnp.where(p < 0, total + 2, p + 1)] = s * stride + i * 32
        return 0

    lax.fori_loop(0, sources, fill, 0)

    def move(s, _):
        for i in range(slots):
            p = jnp.maximum(table[s, i], 0)
            a = where[p]
            b = where[p + 2]
            above = x[pl.ds(pl.multiple_of(jnp.maximum(a, 0) + EDGE, EDGE), EDGE)]
            below = x[pl.ds(pl.multiple_of(jnp.maximum(b, 0), EDGE), EDGE)]
            o[s, i * 32 : i * 32 + EDGE] = jnp.where(a >= 0, above, jnp.zeros_like(above))
            o[s, i * 32 + EDGE : i * 32 + 32] = jnp.where(b >= 0, below, jnp.zeros_like(below))
        return 0

    lax.fori_loop(0, sources, move, 0)


def permute(x, slots):
    sources, rows, width = x.shape
    total = sources * (slots // 2)
    return pl.pallas_call(
        functools.partial(permute_kernel, slots),
        out_shape=jax.ShapeDtypeStruct((sources, slots * 32, width), BF16),
        in_specs=[pl.BlockSpec(memory_space=pltpu.VMEM)],
        out_specs=pl.BlockSpec(memory_space=pltpu.VMEM),
        scratch_shapes=[
            pltpu.VMEM((sources, 128), jnp.int32),
            pltpu.SMEM((sources, 128), jnp.int32),
            pltpu.SMEM((total + 3,), jnp.int32),
            pltpu.SemaphoreType.DMA,
        ],
        compiler_params=pltpu.CompilerParams(vmem_limit_bytes=16 * 2**20),
        cost_estimate=cost(0, 2**23),
        name="permute",
    )(x.reshape(sources * rows, width))


def shards(
    shot_traces, slot_dest, slot_offset, block_count, amp_index, amp_table, dip_trace, dip_time
):
    x = shot_traces[0]
    slots, block, samples = x.shape
    count = block_count.reshape(1)

    ends = payload(block_count, slot_dest, slot_offset, x)
    ends = lax.all_to_all(ends, "rline", split_axis=0, concat_axis=0, tiled=True)

    amps = lax.all_gather(amp_table, "shot", axis=0, tiled=True)
    table_hit = amp_index[0][:, :, None] == jnp.arange(amps.shape[0], dtype=jnp.int32)
    weight = jnp.sum(jnp.where(table_hit, amps, F32(0.0)), axis=2)[:, None]

    out = interior(count, x, weight, dip_trace, dip_time, 0, FIRST)
    ends, out = lax.optimization_barrier((ends, out))
    moved = permute(ends, slots)
    halo = lax.all_to_all(moved, "rline", split_axis=0, concat_axis=0, tiled=True)
    out = interior(count, x, weight, dip_trace, dip_time, FIRST, slots - FIRST, out)
    out = edges(count, x, halo, weight, dip_trace, dip_time, out)
    return out[None]


def solution(mesh):
    in_specs = (
        P("shot", "rline", None, None),
        P("shot", "rline"),
        P("shot", "rline"),
        P("shot", "rline"),
        P("shot", "rline", None),
        P("shot"),
        P(),
        P(),
    )
    out_specs = P("shot", "rline", None, None)
    return jax.shard_map(shards, mesh=mesh, in_specs=in_specs, out_specs=out_specs, check_vma=False)
```
